32 devices in a mesh: region: 4 (over y, core), local: 8 (over z, x).
Axes of the slice: x: 2, y: 2, z: 4, core: 2. Of those that a mesh axis runs over, the one named last changes fastest.
Arguments:
- block_flags: int32 [32, 192], P(None, ('region', 'local')), may hold values 0 or 1
- trace: bfloat16 [32, 24576], P(None, ('region', 'local')), may hold values from 0.099609375 to 1
- w_region: bfloat16 [4, 6144, 6144], P('region', None, 'local'), may hold values from -0.078125 to 0.078125
- lr_weight: bfloat16 [4, 8, 4, 8, 128, 128], P('region', 'local'), may hold values from -0.1875 to 0.1875
- lr_source: int32 [4, 8, 4, 8], P('region', 'local'), may hold values from 0 to 5
- lr_target: int32 [4, 8, 4, 8], P('region', 'local'), may hold values from 0 to 47
- lr_count: int32 [4, 8, 4], P('region', 'local'), may hold values from 0 to 8, as said below
- g_decay: float32 [24576], P(('region', 'local')), may hold values from 0.5 to 0.97
- v_decay: float32 [24576], P(('region', 'local')), may hold values from 0.4 to 0.95
- g_start: float32 [24576], P(('region', 'local')), may hold values from -6 to 6
- v_start: float32 [24576], P(('region', 'local')), may hold values from -6 to 6
Outputs:
- membrane: float32 [32, 24576], P(None, ('region', 'local'))
- g_final: float32 [24576], P(('region', 'local'))
The draws below stay inside these ranges and needn't reach their ends.
Inputs may be any that keep to these rules, and one draw needn't show every extreme that they name: lr_count is 0 for a region's own devices, exactly 8 from every device to the next region (d = (r + 1) % 4), and 1 to 8 otherwise.
All inputs are finite; a program needn't handle non-finite values. No bound on the sum of `block_flags` on one device may be relied on, other than what follows from the above.
Results may differ from the reference program's by a relative error of at most 0.0003.
Values may be sent and summed in bfloat16 or wider, within the bound.
No kernel may reach another device: no remote copies, remote signals or barrier semaphores. Data moves between devices by JAX's collectives and lax.ppermute only.
A program may use at most 128 MiB of HBM per device.

```python
import math
import jax
import jax.numpy as jnp
from jax import lax

B = 128
NB_DEV = 6
STEPS = 32
CAP = 8
REGIONS = 4
LOCALS = 8
BLOCKS_REGION = 48
ALLBLOCKS = 192
NEURONS = 24576


def draw_lr_count(key, part):
    shape = (REGIONS, LOCALS, REGIONS)
    source_region = jax.lax.broadcasted_iota(jnp.int32, shape, 0)
    dest_region = jax.lax.broadcasted_iota(jnp.int32, shape, 2)
    counts = jax.random.randint(jax.random.fold_in(key, 17), shape, 1, CAP + 1).astype(jnp.int32)
    counts = jnp.where(dest_region == (source_region + 1) % REGIONS, CAP, counts)
    counts = jnp.where(dest_region == source_region, 0, counts)
    return counts.astype(jnp.int32)


def place_ends(array, own_key, smallest, largest):
    place = [jax.random.randint(jax.random.fold_in(own_key, axis), (), 0, length) for axis, length in enumerate(array.shape)]
    main_axis = array.shape.index(max(array.shape))
    neighbour = place[:main_axis] + [(place[main_axis] + 1) % array.shape[main_axis]] + place[main_axis + 1:]
    return array.at[tuple(place)].set(smallest).at[tuple(neighbour)].set(largest)


def block_levels(rng, extent, cuts, smallest, top_value):
    loudness, own = 1.0, jax.random.fold_in(rng, 6)
    for dim, shards_of in cuts:
        draws = jnp.exp(jax.random.uniform(jax.random.fold_in(own, dim), (shards_of,), jnp.float32, smallest / len(cuts), top_value / len(cuts)))
        loudness = loudness * jnp.repeat(draws, extent[dim] // shards_of).reshape([-1 if axis == dim else 1 for axis in range(len(extent))])
    return loudness


def noise(key, shape, width, most, pieces=(), held_as=jnp.bfloat16):
    gain = block_levels(key, shape, pieces, -0.22, 0.18) if pieces else 1.0
    values = jax.random.normal(key, shape, jnp.float32) * width * gain
    return jnp.minimum(jnp.maximum(values, -most), most).astype(held_as)


def setup_inputs(seed: int = 0) -> dict:
    key_of = jax.random.split(jax.random.key(seed), 12)
    block_flags = place_ends((jax.random.randint(key_of[0], (STEPS, ALLBLOCKS), 0, 2) < 1).astype(jnp.int32), jax.random.fold_in(key_of[0], 1), 0, 1)
    trace = jnp.clip(jnp.exp(math.log(1.0) - 2.306499 * jax.random.uniform(key_of[1], (STEPS, NEURONS), jnp.float32) ** block_levels(key_of[1], (STEPS, NEURONS), ((1, 32),), -0.2, 0.2)), 0.099609375, 1.0).astype(jnp.bfloat16)
    w_region = noise(key_of[2], (REGIONS, BLOCKS_REGION * B, BLOCKS_REGION * B), (BLOCKS_REGION * B) ** -0.5, 0.078125, ((0, 4), (2, 8)))
    lr_weight = noise(key_of[3], (REGIONS, LOCALS, REGIONS, CAP, B, B), (B * CAP) ** -0.5, 0.1875, ((0, 4), (1, 8)))
    lr_source = place_ends(jax.random.randint(key_of[4], (REGIONS, LOCALS, REGIONS, CAP), 0, NB_DEV), jax.random.fold_in(key_of[4], 1), 0, NB_DEV - 1).astype(jnp.int32)
    lr_target = place_ends(jax.random.randint(key_of[5], (REGIONS, LOCALS, REGIONS, CAP), 0, BLOCKS_REGION), jax.random.fold_in(key_of[5], 1), 0, BLOCKS_REGION - 1).astype(jnp.int32)
    lr_count = draw_lr_count(jax.random.fold_in(key_of[11], 71), 0)
    g_decay = jnp.clip(jnp.exp(math.log(0.97) - 0.662688 * jax.random.uniform(key_of[7], (NEURONS,), jnp.float32) ** block_levels(key_of[7], (NEURONS,), ((0, 32),), -0.2, 0.2)), 0.5, 0.97)
    v_decay = jnp.clip(jnp.exp(math.log(0.95) - 0.8649974 * jax.random.uniform(key_of[8], (NEURONS,), jnp.float32) ** block_levels(key_of[8], (NEURONS,), ((0, 32),), -0.2, 0.2)), 0.4, 0.95)
    g_start = noise(key_of[9], (NEURONS,), 1.0, 6.0, ((0, 32),), jnp.float32)
    v_start = noise(key_of[10], (NEURONS,), 1.0, 6.0, ((0, 32),), jnp.float32)
    return dict(block_flags=block_flags, trace=trace, w_region=w_region, lr_weight=lr_weight, lr_source=lr_source, lr_target=lr_target, lr_count=lr_count, g_decay=g_decay, v_decay=v_decay, g_start=g_start, v_start=v_start)


def reference(block_flags, trace, w_region, lr_weight, lr_source, lr_target, lr_count, g_decay, v_decay, g_start, v_start):
    flags = jnp.repeat(block_flags, B, axis=1).astype(jnp.bfloat16)
    drive = (flags * trace).astype(jnp.bfloat16)
    by_region = drive.reshape(STEPS, REGIONS, BLOCKS_REGION * B).transpose(1, 0, 2)

    def region_product(pair):
        return jnp.dot(pair[0], pair[1], preferred_element_type=jnp.float32)

    inner = lax.map(region_product, (by_region, w_region))
    inner = inner.transpose(1, 0, 2).reshape(STEPS, NEURONS)

    blocks = drive.reshape(STEPS, REGIONS, LOCALS, NB_DEV, B).transpose(1, 2, 3, 0, 4)
    chosen = jax.vmap(jax.vmap(lambda blk, src: blk[src]))(blocks, lr_source)
    partial_value = jnp.einsum('rldcsi,rldcio->rldcso', chosen.astype(jnp.float32), lr_weight.astype(jnp.float32))
    live = (jnp.arange(CAP, dtype=jnp.int32)[None, None, None, :] < lr_count[:, :, :, None]).astype(jnp.float32)
    partial_value = partial_value * live[:, :, :, :, None, None]
    onehot = (lr_target[..., None] == jnp.arange(BLOCKS_REGION, dtype=jnp.int32)).astype(jnp.float32)
    flat = partial_value.reshape(REGIONS, LOCALS, REGIONS, CAP, STEPS * B)
    outer = jnp.einsum('rldcb,rldcx->dbx', onehot, flat, precision=lax.Precision.HIGHEST)
    outer = outer.reshape(REGIONS, BLOCKS_REGION, STEPS, B).transpose(2, 0, 1, 3).reshape(STEPS, NEURONS)
    current = inner + outer

    def advance(carry, now):
        g_state, v_state = carry
        g_state = g_decay * g_state + (1.0 - g_decay) * now
        v_state = v_decay * v_state + (1.0 - v_decay) * g_state
        return (g_state, v_state), v_state

    (g_last, v_last), membrane = lax.scan(advance, (g_start, v_start), current)
    return membrane, g_last
```

```python
import functools

import jax
import jax.numpy as jnp
from jax import lax
from jax.experimental import pallas as pl
from jax.experimental.pallas import tpu as pltpu
from jax.sharding import PartitionSpec as P

TOP = 32766.0
VMEM = pl.BlockSpec(memory_space=pltpu.VMEM)
SMEM = pl.BlockSpec(memory_space=pltpu.SMEM)
ANY = pl.BlockSpec(memory_space=pl.ANY)


def code(value):
    most = jnp.max(jnp.abs(value), axis=-1, keepdims=True)
    power = jnp.ceil(jnp.log2(jnp.maximum(most, 1e-30)) + 1e-5)
    whole = jnp.round(value * (jnp.exp2(-power) * TOP))
    whole = jnp.clip(whole, -32767.0, 32767.0)
    return whole.astype(jnp.int32).astype(jnp.int16), power


def partial_kernel(
    regions, halves, per_half, flags, trace, source, target, count, weight, drive, *rest
):
    outs = rest[: regions - 1]
    tiles, blocks, sem = rest[regions - 1 :]
    steps = trace.shape[0]
    own_blocks, _, width = blocks.shape
    slots = source.shape[1]
    region = lax.axis_index("region")
    copies = []
    for k in range(1, regions):
        copy = pltpu.make_async_copy(weight.at[region ^ k], tiles.at[k - 1], sem.at[k - 1])
        copy.start()
        copies.append(copy)
    for b in range(own_blocks):
        cols = slice(b * width, (b + 1) * width)
        block = (trace[:, cols].astype(jnp.float32) * flags[:, b : b + 1].astype(jnp.float32)).astype(
            jnp.bfloat16
        )
        blocks[b] = block
        for l in range(drive.shape[0]):
            drive[l, :, cols] = block
    lane = lax.broadcasted_iota(jnp.int32, (steps, width), 1)
    for k in range(1, regions):
        copies[k - 1].wait()
        dest = region ^ k
        live = count[0, dest]
        meta = jnp.zeros((steps, width), jnp.int32)
        for j in range(slots):
            part = jnp.dot(
                blocks[source[dest, j]], tiles[k - 1, j], preferred_element_type=jnp.float32
            )
            whole, power = code(part)
            outs[k - 1][j] = whole
            block = target[dest, j]
            owner = block // own_blocks
            place = (
                (owner % halves) * per_half
                + (owner // halves) * own_blocks
                + block
                - owner * own_blocks
            )
            place = jnp.where(j < live, place, -1)
            meta = jnp.where(lane == j, power.astype(jnp.int32), meta)
            meta = jnp.where(lane == slots + j, place, meta)
        outs[k - 1][slots] = meta.astype(jnp.int16)


def gather_kernel(n_in, n_far, halves, own_blocks, *refs):
    ins = refs[:n_in]
    outs = refs[n_in : n_in + n_far - 1]
    own, total, ids, ids_s, sem = refs[n_in + n_far - 1 :]
    slots = ins[0].shape[0] - 1
    steps, width = ins[0].shape[1:]
    per_half = n_far * own_blocks
    local = lax.axis_index("local")
    half = local % halves
    far = local // halves
    for p in range(n_in):
        ids[p] = ins[p][slots, 0:16].astype(jnp.int32)[0:8]
    copy = pltpu.make_async_copy(ids, ids_s, sem)
    copy.start()
    total[...] = jnp.zeros_like(total)
    copy.wait()
    for p in range(n_in):
        scale = jnp.exp2(ins[p][slots].astype(jnp.float32)) * (1.0 / TOP)
        for j in range(slots):
            place = ids_s[p, 0, slots + j] - half * per_half
            place = jnp.where((place >= 0) & (place < per_half), place, per_half)
            total[place] += ins[p][j].astype(jnp.float32) * scale[:, j : j + 1]
    lane = lax.broadcasted_iota(jnp.int32, (steps, width), 1)
    for i in range(own_blocks):
        own[i] = total[far * own_blocks + i]
    for k in range(1, n_far):
        meta = jnp.zeros((steps, width), jnp.int32)
        for i in range(own_blocks):
            whole, power = code(total[(far ^ k) * own_blocks + i])
            outs[k - 1][i] = whole
            meta = jnp.where(lane == i, power.astype(jnp.int32), meta)
        outs[k - 1][own_blocks] = meta.astype(jnp.int16)


def inner_kernel(drive, weight, out):
    @pl.when(pl.program_id(0) == 0)
    def _():
        out[...] = jnp.zeros_like(out)

    out[...] += jnp.dot(drive[0], weight[...], preferred_element_type=jnp.float32)


def advance_kernel(n_in, inner, own, *refs):
    ins = refs[:n_in]
    g_decay, v_decay, g_start, v_start, membrane, g_last, current = refs[n_in:]
    own_blocks, steps, width = own.shape
    scales = [jnp.exp2(r[own_blocks].astype(jnp.float32)) * (1.0 / TOP) for r in ins]
    for i in range(own_blocks):
        cols = slice(i * width, (i + 1) * width)
        value = inner[:, cols] + own[i]
        for r, scale in zip(ins, scales):
            value += r[i].astype(jnp.float32) * scale[:, i : i + 1]
        current[:, cols] = value
    a, b = g_decay[...], v_decay[...]
    g, v = g_start[...], v_start[...]
    for t in range(steps):
        g = a * g + (1.0 - a) * current[t : t + 1, :]
        v = b * v + (1.0 - b) * g
        membrane[t : t + 1, :] = v
    g_last[...] = g


def local(
    regions,
    locals_,
    block_flags,
    trace,
    w_region,
    lr_weight,
    lr_source,
    lr_target,
    lr_count,
    g_decay,
    v_decay,
    g_start,
    v_start,
):
    steps = trace.shape[0]
    own_blocks = block_flags.shape[1]
    neurons = trace.shape[1]
    width = neurons // own_blocks
    slots = lr_target.shape[3]
    halves = 2
    n_far = locals_ // halves
    per_half = n_far * own_blocks
    f32, i16 = jnp.float32, jnp.int16
    sent = jax.ShapeDtypeStruct((slots + 1, steps, width), i16)
    drive, *parts = pl.pallas_call(
        functools.partial(partial_kernel, regions, halves, per_half),
        out_shape=[jax.ShapeDtypeStruct((locals_, steps, neurons), jnp.bfloat16)]
        + [sent] * (regions - 1),
        in_specs=[VMEM, VMEM, SMEM, SMEM, SMEM, ANY],
        out_specs=[VMEM] * regions,
        scratch_shapes=[
            pltpu.VMEM((regions - 1, slots, width, width), jnp.bfloat16),
            pltpu.VMEM((own_blocks, steps, width), jnp.bfloat16),
            pltpu.SemaphoreType.DMA((regions - 1,)),
        ],
        compiler_params=pltpu.CompilerParams(vmem_limit_bytes=16 << 20),
        name="partials",
    )(block_flags, trace, lr_source[0, 0], lr_target[0, 0], lr_count[0], lr_weight[0, 0])

    arrived = []
    for k in range(regions - 1, 0, -1):
        for h in range(halves - 1, -1, -1):
            pairs = [
                (r * locals_ + l, (r ^ k) * locals_ + (l ^ h))
                for r in range(regions)
                for l in range(locals_)
            ]
            arrived.append(lax.ppermute(parts[k - 1], ("region", "local"), pairs))
    drives = lax.all_to_all(drive, "local", split_axis=0, concat_axis=0, tiled=True)

    n_in = len(arrived)
    far_sent = jax.ShapeDtypeStruct((own_blocks + 1, steps, width), i16)
    *sums, own = pl.pallas_call(
        functools.partial(gather_kernel, n_in, n_far, halves, own_blocks),
        out_shape=[far_sent] * (n_far - 1)
        + [jax.ShapeDtypeStruct((own_blocks, steps, width), f32)],
        in_specs=[VMEM] * n_in,
        out_specs=[VMEM] * n_far,
        scratch_shapes=[
            pltpu.VMEM((per_half + 1, steps, width), f32),
            pltpu.VMEM((n_in, 8, width), jnp.int32),
            pltpu.SMEM((n_in, 8, width), jnp.int32),
            pltpu.SemaphoreType.DMA,
        ],
        compiler_params=pltpu.CompilerParams(vmem_limit_bytes=16 << 20),
        name="add_arrived",
    )(*arrived)

    far = [
        lax.ppermute(sums[k - 1], "local", [(l, l ^ (k * halves)) for l in range(locals_)])
        for k in range(1, n_far)
    ]

    inner = pl.pallas_call(
        inner_kernel,
        grid=(locals_,),
        out_shape=jax.ShapeDtypeStruct((steps, neurons), f32),
        in_specs=[
            pl.BlockSpec((1, steps, neurons), lambda l: (l, 0, 0)),
            pl.BlockSpec((neurons, neurons), lambda l: (l, 0)),
        ],
        out_specs=pl.BlockSpec((steps, neurons), lambda l: (0, 0)),
        compiler_params=pltpu.CompilerParams(vmem_limit_bytes=16 << 20),
        cost_estimate=pl.CostEstimate(
            flops=2 * steps * neurons * neurons * locals_,
            bytes_accessed=2 * neurons * neurons * locals_,
            transcendentals=0,
        ),
        name="inner",
    )(drives, w_region[0])

    row = lambda x: x.reshape(1, neurons)
    membrane, g_last = pl.pallas_call(
        functools.partial(advance_kernel, n_far - 1),
        out_shape=[
            jax.ShapeDtypeStruct((steps, neurons), f32),
            jax.ShapeDtypeStruct((1, neurons), f32),
        ],
        in_specs=[VMEM] * (n_far + 5),
        out_specs=[VMEM] * 2,
        scratch_shapes=[pltpu.VMEM((steps, neurons), f32)],
        compiler_params=pltpu.CompilerParams(vmem_limit_bytes=16 << 20),
        name="advance",
    )(inner, own, *far, row(g_decay), row(v_decay), row(g_start), row(v_start))
    return membrane, g_last.reshape(neurons)


def solution(mesh):
    return jax.shard_map(
        functools.partial(local, mesh.shape["region"], mesh.shape["local"]),
        mesh=mesh,
        in_specs=(
            P(None, ("region", "local")),
            P(None, ("region", "local")),
            P("region", None, "local"),
            P("region", "local", None, None, None, None),
            P("region", "local", None, None),
            P("region", "local", None, None),
            P("region", "local", None),
            P(("region", "local")),
            P(("region", "local")),
            P(("region", "local")),
            P(("region", "local")),
        ),
        out_specs=(P(None, ("region", "local")), P(("region", "local"))),
        check_vma=False,
    )
```

```python
import functools

import jax
import jax.numpy as jnp
from jax import lax
from jax.experimental import pallas as pl
from jax.experimental.pallas import tpu as pltpu
from jax.sharding import PartitionSpec as P

TOP = 32766.0
VMEM = pl.BlockSpec(memory_space=pltpu.VMEM)
HBM = pl.BlockSpec(memory_space=pltpu.HBM)
PARAMS = pltpu.CompilerParams(vmem_limit_bytes=24 << 20)
CORES = 2
HALVES = 2


def code(value):
    most = jnp.max(jnp.abs(value), axis=-1, keepdims=True)
    power = jnp.ceil(jnp.log2(jnp.maximum(most, 1e-30)) + 1e-5)
    whole = jnp.round(value * (jnp.exp2(-power) * TOP))
    whole = jnp.clip(whole, -32767.0, 32767.0)
    return whole.astype(jnp.int32).astype(jnp.int16), power


def scales_of(meta):
    return jnp.exp2(meta.astype(jnp.float32)) * (1.0 / TOP)


def load_all(pairs, sems):
    copies = [pltpu.make_async_copy(a, b, sems.at[i]) for i, (a, b) in enumerate(pairs)]
    for copy in copies:
        copy.start()
    return copies


def send_slots(dest, blocks, tiles, source, target, count, per_half, out):
    own_blocks, steps, width = blocks.shape
    slots = source.shape[1]
    lane = lax.broadcasted_iota(jnp.int32, (steps, width), 1)
    live = count[0, dest]
    meta = jnp.zeros((steps, width), jnp.int32)
    for j in range(slots):
        part = jnp.dot(blocks[source[dest, j]], tiles[j], preferred_element_type=jnp.float32)
        whole, power = code(part)
        out[j] = whole
        block = target[dest, j]
        owner = block // own_blocks
        place = (
            (owner % HALVES) * per_half
            + (owner // HALVES) * own_blocks
            + block
            - owner * own_blocks
        )
        place = jnp.where(j < live, place, -1)
        meta = jnp.where(lane == j, power.astype(jnp.int32), meta)
        meta = jnp.where(lane == slots + j, place, meta)
    out[slots] = meta.astype(jnp.int16)


def first_kernel(
    per_half,
    flags_h,
    trace_h,
    source_h,
    target_h,
    count_h,
    weight,
    drive,
    out,
    flags,
    trace,
    source,
    target,
    count,
    tiles,
    sems,
):
    n = out.shape[0]
    own_blocks, steps, width = drive.shape
    region = lax.axis_index("region")
    copies = load_all(
        [(flags_h, flags), (trace_h, trace), (source_h, source), (target_h, target), (count_h, count)]
        + [(weight.at[region ^ 1 ^ (CORES * k)], tiles.at[k]) for k in range(n)],
        sems,
    )
    for copy in copies[:5]:
        copy.wait()
    row = lax.broadcasted_iota(jnp.int32, (steps, steps), 0)
    col = lax.broadcasted_iota(jnp.int32, (steps, steps), 1)
    for b in range(own_blocks):
        across = jnp.where(row == col, flags[b : b + 1, :], 0).astype(jnp.float32)
        on = jnp.sum(across, axis=1, keepdims=True)
        part = trace[:, b * width : (b + 1) * width].astype(jnp.float32)
        drive[b] = (part * on).astype(jnp.bfloat16)
    for k in range(n):
        copies[5 + k].wait()
        dest = region ^ 1 ^ (CORES * k)
        send_slots(dest, drive, tiles.at[k], source, target, count, per_half, out.at[k])


def second_kernel(
    per_half, drive, source_h, target_h, count_h, weight, out, source, target, count, tiles, sems
):
    n = out.shape[0]
    region = lax.axis_index("region")
    copies = load_all(
        [(source_h, source), (target_h, target), (count_h, count)]
        + [(weight.at[region ^ (CORES * (k + 1))], tiles.at[k]) for k in range(n)],
        sems,
    )
    for copy in copies[:3]:
        copy.wait()
    for k in range(n):
        copies[3 + k].wait()
        dest = region ^ (CORES * (k + 1))
        send_slots(dest, drive, tiles.at[k], source, target, count, per_half, out.at[k])


def merge_kernel(n, sibling, mine, drive, drive_x, *outs):
    for k in range(n):
        outs[k][0] = mine[k]
        outs[k][1] = sibling[k + 1]
    outs[n][...] = sibling[0]
    half = lax.axis_index("local") % HALVES
    outs[n + 1][half] = drive[...]
    outs[n + 1][1 - half] = drive_x[...]


def gather_kernel(n_in, n_far, own_blocks, *refs):
    ins = refs[:n_in]
    outs = refs[n_in : n_in + n_far - 1]
    own, total, ids, ids_s, sem = refs[n_in + n_far - 1 :]
    packs = []
    for r in ins:
        packs += [r] if len(r.shape) == 3 else [r.at[i] for i in range(r.shape[0])]
    slots = packs[0].shape[0] - 1
    steps, width = packs[0].shape[1:]
    per_half = n_far * own_blocks
    local = lax.axis_index("local")
    half = local % HALVES
    far = local // HALVES
    for p, pack in enumerate(packs):
        ids[p] = pack[slots, 0:16].astype(jnp.int32)[0:8]
    copy = pltpu.make_async_copy(ids, ids_s, sem)
    copy.start()
    total[...] = jnp.zeros_like(total)
    copy.wait()
    for p, pack in enumerate(packs):
        scale = scales_of(pack[slots])
        for j in range(slots):
            place = ids_s[p, 0, slots + j] - half * per_half
            place = jnp.where((place >= 0) & (place < per_half), place, per_half)
            total[place] += pack[j].astype(jnp.float32) * scale[:, j : j + 1]
    lane = lax.broadcasted_iota(jnp.int32, (steps, width), 1)
    for i in range(own_blocks):
        own[i] = total[far * own_blocks + i]
    for k in range(1, n_far):
        meta = jnp.zeros((steps, width), jnp.int32)
        for i in range(own_blocks):
            whole, power = code(total[(far ^ k) * own_blocks + i])
            outs[k - 1][i] = whole
            meta = jnp.where(lane == i, power.astype(jnp.int32), meta)
        outs[k - 1][own_blocks] = meta.astype(jnp.int16)


def inner_kernel(n_far, *refs):
    pairs = refs[:n_far]
    weight, out, held, sems = refs[n_far:]
    halves, own_blocks, steps, width = pairs[0].shape
    depth = own_blocks * width
    far = lax.axis_index("local") // HALVES
    copies = load_all(
        [
            (
                weight.at[pl.ds(pl.multiple_of(((far ^ k) * halves + h) * depth, depth), depth)],
                held.at[k * halves + h],
            )
            for k in range(n_far)
            for h in range(halves)
        ],
        sems,
    )
    total = jnp.zeros(out.shape, jnp.float32)
    for k in range(n_far):
        for h in range(halves):
            left = jnp.concatenate([pairs[k][h, b] for b in range(own_blocks)], axis=1)
            copies[k * halves + h].wait()
            total += jnp.dot(left, held[k * halves + h], preferred_element_type=jnp.float32)
    out[...] = total


def advance_kernel(n_in, inner, own, *refs):
    ins = refs[:n_in]
    g_decay, v_decay, g_start, v_start, membrane, g_last, current = refs[n_in:]
    own_blocks, steps, width = own.shape
    scales = [scales_of(r[own_blocks]) for r in ins]
    for i in range(own_blocks):
        cols = slice(i * width, (i + 1) * width)
        value = inner[:, cols] + own[i]
        for r, scale in zip(ins, scales):
            value += r[i].astype(jnp.float32) * scale[:, i : i + 1]
        current[:, cols] = value
    neurons = own_blocks * width
    a, b = g_decay[...].reshape(1, neurons), v_decay[...].reshape(1, neurons)
    g, v = g_start[...].reshape(1, neurons), v_start[...].reshape(1, neurons)
    for t in range(steps):
        g = a * g + (1.0 - a) * current[t : t + 1, :]
        v = b * v + (1.0 - b) * g
        membrane[t : t + 1, :] = v
    g_last[...] = g.reshape(neurons)


def local(
    regions,
    locals_,
    block_flags,
    trace,
    w_region,
    lr_weight,
    lr_source,
    lr_target,
    lr_count,
    g_decay,
    v_decay,
    g_start,
    v_start,
):
    steps = trace.shape[0]
    own_blocks = block_flags.shape[1]
    neurons = trace.shape[1]
    width = neurons // own_blocks
    slots = lr_target.shape[3]
    n_far = locals_ // HALVES
    n_hi = regions // CORES
    per_half = n_far * own_blocks
    f32, i16, bf16, i32 = jnp.float32, jnp.int16, jnp.bfloat16, jnp.int32
    shape = jax.ShapeDtypeStruct

    def to(value, k, j):
        pairs = [
            (r * locals_ + l, (r ^ k) * locals_ + (l ^ j))
            for r in range(regions)
            for l in range(locals_)
        ]
        return lax.ppermute(value, ("region", "local"), pairs)

    ids = (lr_source[0, 0], lr_target[0, 0], lr_count[0])
    id_scratch = [
        pltpu.SMEM((regions, slots), i32),
        pltpu.SMEM((regions, slots), i32),
        pltpu.SMEM((1, regions), i32),
    ]
    drive, theirs = pl.pallas_call(
        functools.partial(first_kernel, per_half),
        out_shape=[
            shape((own_blocks, steps, width), bf16),
            shape((n_hi, slots + 1, steps, width), i16),
        ],
        in_specs=[HBM] * 6,
        out_specs=[VMEM] * 2,
        scratch_shapes=[pltpu.VMEM((own_blocks, steps), i32), pltpu.VMEM((steps, neurons), bf16)]
        + id_scratch
        + [pltpu.VMEM((n_hi, slots, width, width), bf16), pltpu.SemaphoreType.DMA((5 + n_hi,))],
        compiler_params=PARAMS,
        name="first_partials",
    )(block_flags.T, trace, *ids, lr_weight[0, 0])
    sibling = to(theirs, 1, 0)
    drive_x = to(drive, 0, 1)
    mine = pl.pallas_call(
        functools.partial(second_kernel, per_half),
        out_shape=shape((n_hi - 1, slots + 1, steps, width), i16),
        in_specs=[VMEM] + [HBM] * 4,
        out_specs=VMEM,
        scratch_shapes=id_scratch
        + [pltpu.VMEM((n_hi - 1, slots, width, width), bf16), pltpu.SemaphoreType.DMA((2 + n_hi,))],
        compiler_params=PARAMS,
        name="second_partials",
    )(drive, *ids, lr_weight[0, 0])
    *merged, beside, pair = pl.pallas_call(
        functools.partial(merge_kernel, n_hi - 1),
        out_shape=[shape((2, slots + 1, steps, width), i16)] * (n_hi - 1)
        + [
            shape((slots + 1, steps, width), i16),
            shape((HALVES, own_blocks, steps, width), bf16),
        ],
        in_specs=[VMEM] * 4,
        out_specs=[VMEM] * (n_hi + 1),
        compiler_params=PARAMS,
        name="merge",
    )(sibling, mine, drive, drive_x)
    arrived = [beside]
    for k in range(1, n_hi):
        for h in range(HALVES):
            arrived.append(to(merged[k - 1], CORES * k, h))
    arrived.append(to(beside, 0, 1))
    far_first = sorted(range(1, n_far), key=lambda k: (k == 1, k))
    pairs = {k: to(pair, 0, k * HALVES) for k in far_first}

    n_packs = 2 + (n_hi - 1) * HALVES * 2
    far_sent = shape((own_blocks + 1, steps, width), i16)
    *sums, own = pl.pallas_call(
        functools.partial(gather_kernel, len(arrived), n_far, own_blocks),
        out_shape=[far_sent] * (n_far - 1) + [shape((own_blocks, steps, width), f32)],
        in_specs=[VMEM] * len(arrived),
        out_specs=[VMEM] * n_far,
        scratch_shapes=[
            pltpu.VMEM((per_half + 1, steps, width), f32),
            pltpu.VMEM((n_packs, 8, width), i32),
            pltpu.SMEM((n_packs, 8, width), i32),
            pltpu.SemaphoreType.DMA,
        ],
        compiler_params=PARAMS,
        name="add_arrived",
    )(*arrived)
    far = [to(sums[k - 1], 0, k * HALVES) for k in far_first]

    inner = pl.pallas_call(
        functools.partial(inner_kernel, n_far),
        out_shape=shape((steps, neurons), f32),
        in_specs=[VMEM] * n_far + [HBM],
        out_specs=VMEM,
        scratch_shapes=[
            pltpu.VMEM((locals_, neurons, neurons), bf16),
            pltpu.SemaphoreType.DMA((locals_,)),
        ],
        compiler_params=PARAMS,
        cost_estimate=pl.CostEstimate(
            flops=2 * steps * neurons * neurons * locals_,
            bytes_accessed=2 * neurons * neurons * locals_,
            transcendentals=0,
        ),
        name="inner",
    )(pair, *[pairs[k] for k in range(1, n_far)], w_region[0])

    return pl.pallas_call(
        functools.partial(advance_kernel, n_far - 1),
        out_shape=[shape((steps, neurons), f32), shape((neurons,), f32)],
        in_specs=[VMEM] * (n_far + 5),
        out_specs=[VMEM] * 2,
        scratch_shapes=[pltpu.VMEM((steps, neurons), f32)],
        compiler_params=PARAMS,
        name="advance",
    )(inner, own, *far, g_decay, v_decay, g_start, v_start)


def solution(mesh):
    return jax.shard_map(
        functools.partial(local, mesh.shape["region"], mesh.shape["local"]),
        mesh=mesh,
        in_specs=(
            P(None, ("region", "local")),
            P(None, ("region", "local")),
            P("region", None, "local"),
            P("region", "local", None, None, None, None),
            P("region", "local", None, None),
            P("region", "local", None, None),
            P("region", "local", None),
            P(("region", "local")),
            P(("region", "local")),
            P(("region", "local")),
            P(("region", "local")),
        ),
        out_specs=(P(None, ("region", "local")), P(("region", "local"))),
        check_vma=False,
    )
```

```python
import functools

import jax
import jax.numpy as jnp
from jax import lax
from jax.experimental import pallas as pl
from jax.experimental.pallas import tpu as pltpu
from jax.sharding import PartitionSpec as P

TOP = 32766.0
VMEM = pl.BlockSpec(memory_space=pltpu.VMEM)
HBM = pl.BlockSpec(memory_space=pltpu.HBM)
in_hbm = functools.partial(pltpu.with_memory_space_constraint, memory_space=pltpu.HBM)
PARAMS = pltpu.CompilerParams(vmem_limit_bytes=24 << 20)
CORES = 2
HALVES = 2


def code(value):
    most = jnp.max(jnp.abs(value), axis=-1, keepdims=True)
    power = jnp.ceil(jnp.log2(jnp.maximum(most, 1e-30)) + 1e-5)
    whole = jnp.round(value * (jnp.exp2(-power) * TOP))
    whole = jnp.clip(whole, -32767.0, 32767.0)
    return whole.astype(jnp.int32).astype(jnp.int16), power


def scales_of(meta):
    return jnp.exp2(meta.astype(jnp.float32)) * (1.0 / TOP)


def load_all(pairs, sems):
    copies = [pltpu.make_async_copy(a, b, sems.at[i]) for i, (a, b) in enumerate(pairs)]
    for copy in copies:
        copy.start()
    return copies


def choose(dest, blocks, source, target, count, per_half, chosen):
    own_blocks, steps, width = blocks.shape
    slots = source.shape[1]
    lane = lax.broadcasted_iota(jnp.int32, (steps, width), 1)
    live = count[0, dest]
    meta = jnp.zeros((steps, width), jnp.int32)
    for j in range(slots):
        chosen[j] = blocks[source[dest, j]]
        block = target[dest, j]
        owner = block // own_blocks
        place = (
            (owner % HALVES) * per_half
            + (owner // HALVES) * own_blocks
            + block
            - owner * own_blocks
        )
        place = jnp.where(j < live, place, -1)
        meta = jnp.where(lane == slots + j, place, meta)
    return meta


def send_slots(chosen, tiles, meta, out):
    slots, steps, width = chosen.shape
    lane = lax.broadcasted_iota(jnp.int32, (steps, width), 1)
    for j in range(slots):
        part = jnp.dot(chosen[j], tiles[j], preferred_element_type=jnp.float32)
        whole, power = code(part)
        out[j] = whole
        meta = jnp.where(lane == j, power.astype(jnp.int32), meta)
    out[slots] = meta.astype(jnp.int16)


def first_kernel(
    per_half,
    flags_h,
    trace_h,
    source_h,
    target_h,
    count_h,
    weight,
    drive,
    out,
    next_tiles,
    next_chosen,
    next_meta,
    flags,
    trace,
    source,
    target,
    count,
    tiles,
    chosen,
    sems,
):
    n = out.shape[0]
    own_blocks, steps, width = drive.shape
    region = lax.axis_index("region")
    copies = load_all(
        [(flags_h, flags), (trace_h, trace), (source_h, source), (target_h, target), (count_h, count)]
        + [(weight.at[region ^ 1 ^ (CORES * k)], tiles.at[k]) for k in range(n)]
        + [(weight.at[region ^ (CORES * (k + 1))], next_tiles.at[k]) for k in range(n - 1)],
        sems,
    )
    for copy in copies[:5]:
        copy.wait()
    row = lax.broadcasted_iota(jnp.int32, (steps, steps), 0)
    col = lax.broadcasted_iota(jnp.int32, (steps, steps), 1)
    for b in range(own_blocks):
        across = jnp.where(row == col, flags[b : b + 1, :], 0).astype(jnp.float32)
        on = jnp.sum(across, axis=1, keepdims=True)
        part = trace[:, b * width : (b + 1) * width].astype(jnp.float32)
        drive[b] = (part * on).astype(jnp.bfloat16)
    for k in range(n - 1):
        next_meta[k] = choose(
            region ^ (CORES * (k + 1)), drive, source, target, count, per_half, next_chosen.at[k]
        )
    metas = [
        choose(region ^ 1 ^ (CORES * k), drive, source, target, count, per_half, chosen.at[k])
        for k in range(n)
    ]
    for k in range(n):
        copies[5 + k].wait()
        send_slots(chosen.at[k], tiles.at[k], metas[k], out.at[k])
    for copy in copies[5 + n :]:
        copy.wait()


def second_kernel(chosen, meta, tiles, out):
    for k in range(out.shape[0]):
        send_slots(chosen.at[k], tiles.at[k], meta[k], out.at[k])


def merge_kernel(n, sibling, mine, drive, drive_x, *outs):
    for k in range(n):
        outs[k][0] = mine[k]
        outs[k][1] = sibling[k + 1]
    outs[n][...] = sibling[0]
    half = lax.axis_index("local") % HALVES
    outs[n + 1][half] = drive[...]
    outs[n + 1][1 - half] = drive_x[...]


def gather_kernel(n_in, n_far, own_blocks, *refs):
    ins = refs[:n_in]
    outs = refs[n_in : n_in + n_far - 1]
    own, total, ids, ids_s, sem = refs[n_in + n_far - 1 :]
    packs = []
    for r in ins:
        packs += [r] if len(r.shape) == 3 else [r.at[i] for i in range(r.shape[0])]
    slots = packs[0].shape[0] - 1
    steps, width = packs[0].shape[1:]
    per_half = n_far * own_blocks
    local = lax.axis_index("local")
    half = local % HALVES
    far = local // HALVES
    for p, pack in enumerate(packs):
        ids[p] = pack[slots, 0:16].astype(jnp.int32)[0:8]
    copy = pltpu.make_async_copy(ids, ids_s, sem)
    copy.start()
    total[...] = jnp.zeros_like(total)
    copy.wait()
    for p, pack in enumerate(packs):
        scale = scales_of(pack[slots])
        for j in range(slots):
            place = ids_s[p, 0, slots + j] - half * per_half
            place = jnp.where((place >= 0) & (place < per_half), place, per_half)
            total[place] += pack[j].astype(jnp.float32) * scale[:, j : j + 1]
    lane = lax.broadcasted_iota(jnp.int32, (steps, width), 1)
    for i in range(own_blocks):
        own[i] = total[far * own_blocks + i]
    for k in range(1, n_far):
        meta = jnp.zeros((steps, width), jnp.int32)
        for i in range(own_blocks):
            whole, power = code(total[(far ^ k) * own_blocks + i])
            outs[k - 1][i] = whole
            meta = jnp.where(lane == i, power.astype(jnp.int32), meta)
        outs[k - 1][own_blocks] = meta.astype(jnp.int16)


def inner_kernel(n_far, *refs):
    pairs = refs[:n_far]
    weight, out, held, sems = refs[n_far:]
    halves, own_blocks, steps, width = pairs[0].shape
    depth = own_blocks * width
    far = lax.axis_index("local") // HALVES
    copies = load_all(
        [
            (
                weight.at[pl.ds(pl.multiple_of(((far ^ k) * halves + h) * depth, depth), depth)],
                held.at[k * halves + h],
            )
            for k in range(n_far)
            for h in range(halves)
        ],
        sems,
    )
    total = jnp.zeros(out.shape, jnp.float32)
    for k in range(n_far):
        for h in range(halves):
            left = jnp.concatenate([pairs[k][h, b] for b in range(own_blocks)], axis=1)
            copies[k * halves + h].wait()
            total += jnp.dot(left, held[k * halves + h], preferred_element_type=jnp.float32)
    out[...] = total


def advance_kernel(n_in, inner, own, *refs):
    ins = refs[:n_in]
    g_decay, v_decay, g_start, v_start, membrane, g_last, current = refs[n_in:]
    own_blocks, steps, width = own.shape
    scales = [scales_of(r[own_blocks]) for r in ins]
    for i in range(own_blocks):
        cols = slice(i * width, (i + 1) * width)
        value = inner[:, cols] + own[i]
        for r, scale in zip(ins, scales):
            value += r[i].astype(jnp.float32) * scale[:, i : i + 1]
        current[:, cols] = value
    neurons = own_blocks * width
    a, b = g_decay[...].reshape(1, neurons), v_decay[...].reshape(1, neurons)
    g, v = g_start[...].reshape(1, neurons), v_start[...].reshape(1, neurons)
    for t in range(steps):
        g = a * g + (1.0 - a) * current[t : t + 1, :]
        v = b * v + (1.0 - b) * g
        membrane[t : t + 1, :] = v
    g_last[...] = g.reshape(neurons)


def local(
    regions,
    locals_,
    block_flags,
    trace,
    w_region,
    lr_weight,
    lr_source,
    lr_target,
    lr_count,
    g_decay,
    v_decay,
    g_start,
    v_start,
):
    steps = trace.shape[0]
    own_blocks = block_flags.shape[1]
    neurons = trace.shape[1]
    width = neurons // own_blocks
    slots = lr_target.shape[3]
    n_far = locals_ // HALVES
    n_hi = regions // CORES
    per_half = n_far * own_blocks
    f32, i16, bf16, i32 = jnp.float32, jnp.int16, jnp.bfloat16, jnp.int32
    shape = jax.ShapeDtypeStruct

    def to(value, k, j):
        pairs = [
            (r * locals_ + l, (r ^ k) * locals_ + (l ^ j))
            for r in range(regions)
            for l in range(locals_)
        ]
        return lax.ppermute(value, ("region", "local"), pairs)

    drive, theirs, *rest = pl.pallas_call(
        functools.partial(first_kernel, per_half),
        out_shape=[
            shape((own_blocks, steps, width), bf16),
            shape((n_hi, slots + 1, steps, width), i16),
            shape((n_hi - 1, slots, width, width), bf16),
            shape((n_hi - 1, slots, steps, width), bf16),
            shape((n_hi - 1, steps, width), i32),
        ],
        in_specs=[HBM] * 6,
        out_specs=[VMEM] * 5,
        scratch_shapes=[
            pltpu.VMEM((own_blocks, steps), i32),
            pltpu.VMEM((steps, neurons), bf16),
            pltpu.SMEM((regions, slots), i32),
            pltpu.SMEM((regions, slots), i32),
            pltpu.SMEM((1, regions), i32),
            pltpu.VMEM((n_hi, slots, width, width), bf16),
            pltpu.VMEM((n_hi, slots, steps, width), bf16),
            pltpu.SemaphoreType.DMA((4 + 2 * n_hi,)),
        ],
        compiler_params=PARAMS,
        name="first_partials",
    )(
        *[
            in_hbm(x)
            for x in (block_flags.T, trace, lr_source[0, 0], lr_target[0, 0], lr_count[0], lr_weight[0, 0])
        ]
    )
    sibling = to(theirs, 1, 0)
    drive_x = to(drive, 0, 1)
    tiles, chosen, meta = rest
    mine = pl.pallas_call(
        second_kernel,
        out_shape=shape((n_hi - 1, slots + 1, steps, width), i16),
        in_specs=[VMEM] * 3,
        out_specs=VMEM,
        compiler_params=PARAMS,
        name="second_partials",
    )(chosen, meta, tiles)
    *merged, beside, pair = pl.pallas_call(
        functools.partial(merge_kernel, n_hi - 1),
        out_shape=[shape((2, slots + 1, steps, width), i16)] * (n_hi - 1)
        + [
            shape((slots + 1, steps, width), i16),
            shape((HALVES, own_blocks, steps, width), bf16),
        ],
        in_specs=[VMEM] * 4,
        out_specs=[VMEM] * (n_hi + 1),
        compiler_params=PARAMS,
        name="merge",
    )(sibling, mine, drive, drive_x)
    arrived = [beside]
    for k in range(1, n_hi):
        for h in range(HALVES):
            arrived.append(to(merged[k - 1], CORES * k, h))
    arrived.append(to(beside, 0, 1))
    far_first = sorted(range(1, n_far), key=lambda k: (k == 1, k))
    pairs = {k: to(pair, 0, k * HALVES) for k in far_first}

    n_packs = 2 + (n_hi - 1) * HALVES * 2
    far_sent = shape((own_blocks + 1, steps, width), i16)
    *sums, own = pl.pallas_call(
        functools.partial(gather_kernel, len(arrived), n_far, own_blocks),
        out_shape=[far_sent] * (n_far - 1) + [shape((own_blocks, steps, width), f32)],
        in_specs=[VMEM] * len(arrived),
        out_specs=[VMEM] * n_far,
        scratch_shapes=[
            pltpu.VMEM((per_half + 1, steps, width), f32),
            pltpu.VMEM((n_packs, 8, width), i32),
            pltpu.SMEM((n_packs, 8, width), i32),
            pltpu.SemaphoreType.DMA,
        ],
        compiler_params=PARAMS,
        name="add_arrived",
    )(*arrived)
    far = [to(sums[k - 1], 0, k * HALVES) for k in far_first]

    inner = pl.pallas_call(
        functools.partial(inner_kernel, n_far),
        out_shape=shape((steps, neurons), f32),
        in_specs=[VMEM] * n_far + [HBM],
        out_specs=VMEM,
        scratch_shapes=[
            pltpu.VMEM((locals_, neurons, neurons), bf16),
            pltpu.SemaphoreType.DMA((locals_,)),
        ],
        compiler_params=PARAMS,
        cost_estimate=pl.CostEstimate(
            flops=2 * steps * neurons * neurons * locals_,
            bytes_accessed=2 * neurons * neurons * locals_,
            transcendentals=0,
        ),
        name="inner",
    )(pair, *[pairs[k] for k in range(1, n_far)], in_hbm(w_region[0]))

    return pl.pallas_call(
        functools.partial(advance_kernel, n_far - 1),
        out_shape=[shape((steps, neurons), f32), shape((neurons,), f32)],
        in_specs=[VMEM] * (n_far + 5),
        out_specs=[VMEM] * 2,
        scratch_shapes=[pltpu.VMEM((steps, neurons), f32)],
        compiler_params=PARAMS,
        name="advance",
    )(inner, own, *far, g_decay, v_decay, g_start, v_start)


def solution(mesh):
    return jax.shard_map(
        functools.partial(local, mesh.shape["region"], mesh.shape["local"]),
        mesh=mesh,
        in_specs=(
            P(None, ("region", "local")),
            P(None, ("region", "local")),
            P("region", None, "local"),
            P("region", "local", None, None, None, None),
            P("region", "local", None, None),
            P("region", "local", None, None),
            P("region", "local", None),
            P(("region", "local")),
            P(("region", "local")),
            P(("region", "local")),
            P(("region", "local")),
        ),
        out_specs=(P(None, ("region", "local")), P(("region", "local"))),
        check_vma=False,
    )
```

```python
import functools

import jax
import jax.numpy as jnp
from jax import lax
from jax.experimental import pallas as pl
from jax.experimental.pallas import tpu as pltpu
from jax.sharding import PartitionSpec as P

TOP = 32766.0
VMEM = pl.BlockSpec(memory_space=pltpu.VMEM)
HBM = pl.BlockSpec(memory_space=pltpu.HBM)
in_hbm = functools.partial(pltpu.with_memory_space_constraint, memory_space=pltpu.HBM)
PARAMS = pltpu.CompilerParams(vmem_limit_bytes=24 << 20)
CORES = 2
HALVES = 2


def code(value):
    most = jnp.max(jnp.abs(value), axis=-1, keepdims=True)
    power = jnp.ceil(jnp.log2(jnp.maximum(most, 1e-30)) + 1e-5)
    whole = jnp.round(value * (jnp.exp2(-power) * TOP))
    whole = jnp.clip(whole, -32767.0, 32767.0)
    return whole.astype(jnp.int32).astype(jnp.int16), power


def scales_of(meta):
    return jnp.exp2(meta.astype(jnp.float32)) * (1.0 / TOP)


def load_all(pairs, sems):
    copies = [pltpu.make_async_copy(a, b, sems.at[i]) for i, (a, b) in enumerate(pairs)]
    for copy in copies:
        copy.start()
    return copies


def choose(dest, blocks, source, target, count, per_half, chosen):
    own_blocks, steps, width = blocks.shape
    slots = source.shape[1]
    lane = lax.broadcasted_iota(jnp.int32, (steps, width), 1)
    live = count[0, dest]
    meta = jnp.zeros((steps, width), jnp.int32)
    for j in range(slots):
        chosen[j] = blocks[source[dest, j]]
        block = target[dest, j]
        owner = block // own_blocks
        place = (
            (owner % HALVES) * per_half
            + (owner // HALVES) * own_blocks
            + block
            - owner * own_blocks
        )
        place = jnp.where(j < live, place, -1)
        meta = jnp.where(lane == slots + j, place, meta)
    return meta


def send_slots(chosen, tiles, meta, out):
    slots, steps, width = chosen.shape
    lane = lax.broadcasted_iota(jnp.int32, (steps, width), 1)
    for j in range(slots):
        part = jnp.dot(chosen[j], tiles[j], preferred_element_type=jnp.float32)
        whole, power = code(part)
        out[j] = whole
        meta = jnp.where(lane == j, power.astype(jnp.int32), meta)
    out[slots] = meta.astype(jnp.int16)


def first_kernel(
    per_half,
    flags_h,
    trace_h,
    source_h,
    target_h,
    count_h,
    weight,
    drive,
    out,
    across,
    next_tiles,
    next_chosen,
    next_meta,
    flags,
    trace,
    source,
    target,
    count,
    tiles,
    chosen,
    sems,
):
    n = out.shape[0]
    own_blocks, steps, width = drive.shape
    region = lax.axis_index("region")
    copies = load_all(
        [(flags_h, flags), (trace_h, trace), (source_h, source), (target_h, target), (count_h, count)]
        + [(weight.at[region ^ 1 ^ (CORES * k)], tiles.at[k]) for k in range(n)]
        + [(weight.at[region ^ (CORES * (k + 1))], next_tiles.at[k]) for k in range(n - 1)],
        sems,
    )
    for copy in copies[:5]:
        copy.wait()
    row = lax.broadcasted_iota(jnp.int32, (steps, steps), 0)
    col = lax.broadcasted_iota(jnp.int32, (steps, steps), 1)
    for b in range(own_blocks):
        spread = jnp.where(row == col, flags[b : b + 1, :], 0).astype(jnp.float32)
        on = jnp.sum(spread, axis=1, keepdims=True)
        part = trace[:, b * width : (b + 1) * width].astype(jnp.float32)
        drive[b] = (part * on).astype(jnp.bfloat16)
    for k in range(n - 1):
        next_meta[k] = choose(
            region ^ (CORES * (k + 1)), drive, source, target, count, per_half, next_chosen.at[k]
        )
    metas = [
        choose(region ^ 1 ^ (CORES * k), drive, source, target, count, per_half, chosen.at[k])
        for k in range(n)
    ]
    for k in range(n):
        copies[5 + k].wait()
        send_slots(chosen.at[k], tiles.at[k], metas[k], out.at[k])
    across[...] = out[0]
    for copy in copies[5 + n :]:
        copy.wait()


def second_kernel(chosen, meta, tiles, out):
    for k in range(out.shape[0]):
        send_slots(chosen.at[k], tiles.at[k], meta[k], out.at[k])


def merge_kernel(n, sibling, mine, *outs):
    for k in range(n):
        outs[k][0] = mine[k]
        outs[k][1] = sibling[k + 1]


def pair_kernel(drive, drive_x, pair):
    half = lax.axis_index("local") % HALVES
    pair[half] = drive[...]
    pair[1 - half] = drive_x[...]


def gather_kernel(n_in, n_far, own_blocks, *refs):
    ins = refs[:n_in]
    outs = refs[n_in : n_in + n_far - 1]
    own, total, ids, ids_s, sem = refs[n_in + n_far - 1 :]
    packs = [ins[0].at[0]]
    for r in ins[1:]:
        packs += [r] if len(r.shape) == 3 else [r.at[i] for i in range(r.shape[0])]
    slots = packs[0].shape[0] - 1
    steps, width = packs[0].shape[1:]
    per_half = n_far * own_blocks
    local = lax.axis_index("local")
    half = local % HALVES
    far = local // HALVES
    for p, pack in enumerate(packs):
        ids[p] = pack[slots, 0:16].astype(jnp.int32)[0:8]
    copy = pltpu.make_async_copy(ids, ids_s, sem)
    copy.start()
    total[...] = jnp.zeros_like(total)
    copy.wait()
    for p, pack in enumerate(packs):
        scale = scales_of(pack[slots])
        for j in range(slots):
            place = ids_s[p, 0, slots + j] - half * per_half
            place = jnp.where((place >= 0) & (place < per_half), place, per_half)
            total[place] += pack[j].astype(jnp.float32) * scale[:, j : j + 1]
    lane = lax.broadcasted_iota(jnp.int32, (steps, width), 1)
    for i in range(own_blocks):
        own[i] = total[far * own_blocks + i]
    for k in range(1, n_far):
        meta = jnp.zeros((steps, width), jnp.int32)
        for i in range(own_blocks):
            whole, power = code(total[(far ^ k) * own_blocks + i])
            outs[k - 1][i] = whole
            meta = jnp.where(lane == i, power.astype(jnp.int32), meta)
        outs[k - 1][own_blocks] = meta.astype(jnp.int16)


def inner_kernel(n_far, order, *refs):
    pairs = refs[:n_far]
    weight, out = refs[n_far:]
    halves, own_blocks, steps, width = pairs[0].shape
    depth = own_blocks * width
    far = lax.axis_index("local") // HALVES
    total = jnp.zeros(out.shape, jnp.float32)
    for k in range(n_far):
        left = jnp.concatenate(
            [pairs[k][h, b] for h in range(halves) for b in range(own_blocks)], axis=1
        )
        rows = pl.ds(pl.multiple_of((far ^ order[k]) * halves * depth, halves * depth), halves * depth)
        total += jnp.dot(left, weight[rows, :], preferred_element_type=jnp.float32)
    out[...] = total


def advance_kernel(n_in, inner, own, *refs):
    ins = refs[:n_in]
    g_decay, v_decay, g_start, v_start, membrane, g_last, current = refs[n_in:]
    own_blocks, steps, width = own.shape
    scales = [scales_of(r[own_blocks]) for r in ins]
    for i in range(own_blocks):
        cols = slice(i * width, (i + 1) * width)
        value = inner[:, cols] + own[i]
        for r, scale in zip(ins, scales):
            value += r[i].astype(jnp.float32) * scale[:, i : i + 1]
        current[:, cols] = value
    neurons = own_blocks * width
    a, b = g_decay[...].reshape(1, neurons), v_decay[...].reshape(1, neurons)
    g, v = g_start[...].reshape(1, neurons), v_start[...].reshape(1, neurons)
    for t in range(steps):
        g = a * g + (1.0 - a) * current[t : t + 1, :]
        v = b * v + (1.0 - b) * g
        membrane[t : t + 1, :] = v
    g_last[...] = g.reshape(neurons)


def local(
    regions,
    locals_,
    block_flags,
    trace,
    w_region,
    lr_weight,
    lr_source,
    lr_target,
    lr_count,
    g_decay,
    v_decay,
    g_start,
    v_start,
):
    steps = trace.shape[0]
    own_blocks = block_flags.shape[1]
    neurons = trace.shape[1]
    width = neurons // own_blocks
    slots = lr_target.shape[3]
    n_far = locals_ // HALVES
    n_hi = regions // CORES
    per_half = n_far * own_blocks
    f32, i16, bf16, i32 = jnp.float32, jnp.int16, jnp.bfloat16, jnp.int32
    shape = jax.ShapeDtypeStruct

    def to(value, k, j):
        pairs = [
            (r * locals_ + l, (r ^ k) * locals_ + (l ^ j))
            for r in range(regions)
            for l in range(locals_)
        ]
        return lax.ppermute(value, ("region", "local"), pairs)

    drive, theirs, across, *rest = pl.pallas_call(
        functools.partial(first_kernel, per_half),
        out_shape=[
            shape((own_blocks, steps, width), bf16),
            shape((n_hi, slots + 1, steps, width), i16),
            shape((slots + 1, steps, width), i16),
            shape((n_hi - 1, slots, width, width), bf16),
            shape((n_hi - 1, slots, steps, width), bf16),
            shape((n_hi - 1, steps, width), i32),
        ],
        in_specs=[HBM] * 6,
        out_specs=[VMEM] * 6,
        scratch_shapes=[
            pltpu.VMEM((own_blocks, steps), i32),
            pltpu.VMEM((steps, neurons), bf16),
            pltpu.SMEM((regions, slots), i32),
            pltpu.SMEM((regions, slots), i32),
            pltpu.SMEM((1, regions), i32),
            pltpu.VMEM((n_hi, slots, width, width), bf16),
            pltpu.VMEM((n_hi, slots, steps, width), bf16),
            pltpu.SemaphoreType.DMA((4 + 2 * n_hi,)),
        ],
        compiler_params=PARAMS,
        name="first_partials",
    )(
        *[
            in_hbm(x)
            for x in (block_flags.T, trace, lr_source[0, 0], lr_target[0, 0], lr_count[0], lr_weight[0, 0])
        ]
    )
    sibling = to(theirs, 1, 0)
    drive_x = to(drive, 0, 1)
    beside = to(across, 1, 1)
    tiles, chosen, meta = rest
    mine = pl.pallas_call(
        second_kernel,
        out_shape=shape((n_hi - 1, slots + 1, steps, width), i16),
        in_specs=[VMEM] * 3,
        out_specs=VMEM,
        compiler_params=PARAMS,
        name="second_partials",
    )(chosen, meta, tiles)
    merged = pl.pallas_call(
        functools.partial(merge_kernel, n_hi - 1),
        out_shape=[shape((2, slots + 1, steps, width), i16)] * (n_hi - 1),
        in_specs=[VMEM] * 2,
        out_specs=[VMEM] * (n_hi - 1),
        compiler_params=PARAMS,
        name="merge",
    )(sibling, mine)
    pair = pl.pallas_call(
        pair_kernel,
        out_shape=shape((HALVES, own_blocks, steps, width), bf16),
        in_specs=[VMEM] * 2,
        out_specs=VMEM,
        compiler_params=PARAMS,
        cost_estimate=pl.CostEstimate(flops=1 << 36, bytes_accessed=1 << 28, transcendentals=1 << 26),
        name="pair",
    )(drive, drive_x)
    arrived = [sibling, beside]
    for k in range(1, n_hi):
        for h in range(HALVES):
            arrived.append(to(merged[k - 1], CORES * k, h))
    drive_order = [2, 3, 1] if n_far == 4 else list(range(1, n_far))
    use_order = [2, 3, 1] if n_far == 4 else list(range(1, n_far))
    sum_order = [2, 3, 1] if n_far == 4 else list(range(1, n_far))
    add_order = [1, 2, 3] if n_far == 4 else list(range(1, n_far))
    pairs = {k: to(pair, 0, k * HALVES) for k in drive_order}

    n_packs = 2 + (n_hi - 1) * HALVES * 2
    far_sent = shape((own_blocks + 1, steps, width), i16)
    *sums, own = pl.pallas_call(
        functools.partial(gather_kernel, len(arrived), n_far, own_blocks),
        out_shape=[far_sent] * (n_far - 1) + [shape((own_blocks, steps, width), f32)],
        in_specs=[VMEM] * len(arrived),
        out_specs=[VMEM] * n_far,
        scratch_shapes=[
            pltpu.VMEM((per_half + 1, steps, width), f32),
            pltpu.VMEM((n_packs, 8, width), i32),
            pltpu.SMEM((n_packs, 8, width), i32),
            pltpu.SemaphoreType.DMA,
        ],
        compiler_params=PARAMS,
        cost_estimate=pl.CostEstimate(flops=1 << 36, bytes_accessed=1 << 28, transcendentals=1 << 26),
        name="add_arrived",
    )(*arrived)
    far = {k: to(sums[k - 1], 0, k * HALVES) for k in sum_order}

    inner = pl.pallas_call(
        functools.partial(inner_kernel, n_far, (0, *use_order)),
        out_shape=shape((steps, neurons), f32),
        in_specs=[VMEM] * (n_far + 1),
        out_specs=VMEM,
        compiler_params=PARAMS,
        cost_estimate=pl.CostEstimate(
            flops=2 * steps * neurons * neurons * locals_,
            bytes_accessed=2 * neurons * neurons * locals_,
            transcendentals=0,
        ),
        name="inner",
    )(pair, *[pairs[k] for k in use_order], w_region[0])

    return pl.pallas_call(
        functools.partial(advance_kernel, n_far - 1),
        out_shape=[shape((steps, neurons), f32), shape((neurons,), f32)],
        in_specs=[VMEM] * (n_far + 5),
        out_specs=[VMEM] * 2,
        scratch_shapes=[pltpu.VMEM((steps, neurons), f32)],
        compiler_params=PARAMS,
        name="advance",
    )(inner, own, *[far[k] for k in add_order], g_decay, v_decay, g_start, v_start)


def solution(mesh):
    return jax.shard_map(
        functools.partial(local, mesh.shape["region"], mesh.shape["local"]),
        mesh=mesh,
        in_specs=(
            P(None, ("region", "local")),
            P(None, ("region", "local")),
            P("region", None, "local"),
            P("region", "local", None, None, None, None),
            P("region", "local", None, None),
            P("region", "local", None, None),
            P("region", "local", None),
            P(("region", "local")),
            P(("region", "local")),
            P(("region", "local")),
            P(("region", "local")),
        ),
        out_specs=(P(None, ("region", "local")), P(("region", "local"))),
        check_vma=False,
    )
```

```python
import functools

import jax
import jax.numpy as jnp
from jax import lax
from jax.experimental import pallas as pl
from jax.experimental.pallas import tpu as pltpu
from jax.sharding import PartitionSpec as P

TOP = 32766.0
VMEM = pl.BlockSpec(memory_space=pltpu.VMEM)
HBM = pl.BlockSpec(memory_space=pltpu.HBM)
in_hbm = functools.partial(pltpu.with_memory_space_constraint, memory_space=pltpu.HBM)
PARAMS = pltpu.CompilerParams(vmem_limit_bytes=24 << 20)
CORES = 2
HALVES = 2
SHIFT = 32


def code(value):
    most = jnp.max(jnp.abs(value), axis=-1, keepdims=True)
    power = jnp.ceil(jnp.log2(jnp.maximum(most, 1e-30)) + 1e-5)
    whole = jnp.round(value * (jnp.exp2(-power) * TOP))
    return whole.astype(jnp.int32).astype(jnp.int16), power.astype(jnp.int32)


def put_power(meta, lane, first, count, j, power):
    half = meta.shape[0]
    meta = jnp.where(lane == first + j, power[:half], meta)
    return jnp.where(lane == first + count + j, power[half:], meta)


def scales_of(meta):
    return jnp.exp2(meta.astype(jnp.float32)) * (1.0 / TOP)


def scale_of(scales, first, count, j):
    upper, lower = first + j, first + count + j
    return jnp.concatenate([scales[:, upper : upper + 1], scales[:, lower : lower + 1]], axis=0)


def load_all(pairs, sems):
    copies = [pltpu.make_async_copy(a, b, sems.at[i]) for i, (a, b) in enumerate(pairs)]
    for copy in copies:
        copy.start()
    return copies


def choose(dest, blocks, source, target, count, per_half, first, chosen):
    own_blocks, steps, width = blocks.shape
    slots = source.shape[1]
    lane = lax.broadcasted_iota(jnp.int32, (steps // 2, width), 1)
    live = count[0, dest]
    meta = jnp.zeros((steps // 2, width), jnp.int32)
    for j in range(slots):
        chosen[j] = blocks[source[dest, j]]
        block = target[dest, j]
        owner = (block * (-(-65536 // own_blocks))) >> 16
        place = (owner % HALVES) * per_half + (owner // HALVES) * own_blocks
        place = jnp.where(j < live, place + block - owner * own_blocks, -1)
        meta = jnp.where(lane == first + 2 * slots + j, place, meta)
    return meta


def send_slots(chosen, tiles, meta, first, out):
    slots, steps, _ = chosen.shape
    lane = lax.broadcasted_iota(jnp.int32, meta.shape, 1)
    for j in range(slots):
        part = jnp.dot(chosen[j], tiles[j], preferred_element_type=jnp.float32)
        whole, power = code(part)
        out[j * steps : (j + 1) * steps] = whole
        meta = put_power(meta, lane, first, slots, j, power)
    out[slots * steps :] = meta.astype(jnp.int16)


def first_kernel(
    per_half,
    flags_h,
    trace_h,
    source_h,
    target_h,
    count_h,
    weight,
    drive,
    out,
    next_tiles,
    next_chosen,
    next_meta,
    flags,
    trace,
    source,
    target,
    count,
    tiles,
    chosen,
    sems,
):
    n = out.shape[0]
    own_blocks, steps, width = drive.shape
    region = lax.axis_index("region")
    copies = load_all(
        [(flags_h, flags), (trace_h, trace), (source_h, source), (target_h, target), (count_h, count)]
        + [(weight.at[region ^ 1 ^ (CORES * k)], tiles.at[k]) for k in range(n)]
        + [(weight.at[region ^ (CORES * (k + 1))], next_tiles.at[k]) for k in range(n - 1)],
        sems,
    )
    for copy in copies[:5]:
        copy.wait()
    row = lax.broadcasted_iota(jnp.int32, (steps, steps), 0)
    col = lax.broadcasted_iota(jnp.int32, (steps, steps), 1)
    for b in range(own_blocks):
        spread = jnp.where(row == col, flags[b : b + 1, :], 0).astype(jnp.float32)
        on = jnp.sum(spread, axis=1, keepdims=True)
        part = trace[:, b * width : (b + 1) * width].astype(jnp.float32)
        drive[b] = (part * on).astype(jnp.bfloat16)
    for k in range(n - 1):
        next_meta[k] = choose(
            region ^ (CORES * (k + 1)), drive, source, target, count, per_half, SHIFT, next_chosen.at[k]
        )
    metas = [
        choose(region ^ 1 ^ (CORES * k), drive, source, target, count, per_half, 0, chosen.at[k])
        for k in range(n)
    ]
    for k in range(n):
        copies[5 + k].wait()
        send_slots(chosen.at[k], tiles.at[k], metas[k], 0, out.at[k])
    for copy in copies[5 + n :]:
        copy.wait()


def second_kernel(chosen, meta, tiles, theirs, out, across):
    across[...] = theirs[0]
    for k in range(out.shape[0]):
        send_slots(chosen.at[k], tiles.at[k], meta[k], SHIFT, out.at[k])


def merge_kernel(n, rows, sibling, mine, *outs):
    for k in range(n):
        outs[k][:rows] = mine[k, :rows]
        outs[k][rows : 2 * rows] = sibling[k + 1, :rows]
        meta = mine[k, rows:].astype(jnp.int32) + sibling[k + 1, rows:].astype(jnp.int32)
        outs[k][2 * rows :] = meta.astype(jnp.int16)


def pair_kernel(drive, drive_x, pair):
    half = lax.axis_index("local") % HALVES
    pair[half] = drive[...]
    pair[1 - half] = drive_x[...]


def add_packs(packs, slots, steps, per_half, total):
    half = lax.axis_index("local") % HALVES
    for ref, row, meta, first in packs:
        block = ref[meta : meta + steps // 2]
        scales = scales_of(block)
        line = block.astype(jnp.int32)[0:1]
        for j in range(slots):
            place = line[0, first + 2 * slots + j] - half * per_half
            place = jnp.where((place >= 0) & (place < per_half), place, per_half)
            rows = ref[row + j * steps : row + (j + 1) * steps].astype(jnp.float32)
            total[place] += rows * scale_of(scales, first, slots, j)


def early_kernel(slots, sibling, beside, total):
    steps = total.shape[1]
    total[...] = jnp.zeros_like(total)
    packs = [(sibling.at[0], 0, slots * steps, 0), (beside, 0, slots * steps, 0)]
    add_packs(packs, slots, steps, total.shape[0] - 1, total)


def late_kernel(n_in, n_far, slots, own_blocks, early, *refs):
    ins = refs[:n_in]
    outs = refs[n_in : n_in + n_far - 1]
    own, total = refs[n_in + n_far - 1 :]
    steps, width = total.shape[1:]
    far = lax.axis_index("local") // HALVES
    total[...] = early[...]
    packs = []
    for r in ins:
        packs += [(r, 0, 2 * slots * steps, SHIFT), (r, slots * steps, 2 * slots * steps, 0)]
    add_packs(packs, slots, steps, n_far * own_blocks, total)
    lane = lax.broadcasted_iota(jnp.int32, (steps // 2, width), 1)
    for i in range(own_blocks):
        own[i] = total[far * own_blocks + i]
    for k in range(1, n_far):
        meta = jnp.zeros((steps // 2, width), jnp.int32)
        for i in range(own_blocks):
            whole, power = code(total[(far ^ k) * own_blocks + i])
            outs[k - 1][i * steps : (i + 1) * steps] = whole
            meta = put_power(meta, lane, 0, own_blocks, i, power)
        outs[k - 1][own_blocks * steps :] = meta.astype(jnp.int16)


def inner_kernel(n_far, order, *refs):
    pairs = refs[:n_far]
    weight, out = refs[n_far:]
    halves, own_blocks, steps, width = pairs[0].shape
    depth = own_blocks * width
    far = lax.axis_index("local") // HALVES
    total = jnp.zeros((steps, depth), jnp.float32)
    for k in range(n_far):
        left = jnp.concatenate(
            [pairs[k][h, b] for h in range(halves) for b in range(own_blocks)], axis=1
        )
        rows = pl.ds(pl.multiple_of((far ^ order[k]) * halves * depth, halves * depth), halves * depth)
        total += jnp.dot(left, weight[rows, :], preferred_element_type=jnp.float32)
    for b in range(own_blocks):
        out[b] = total[:, b * width : (b + 1) * width]


def advance_kernel(n_in, inner, own, *refs):
    ins = refs[:n_in]
    g_decay, v_decay, g_start, v_start, membrane, g_last, current = refs[n_in:]
    own_blocks, steps, width = own.shape
    neurons = own_blocks * width
    a, b = g_decay[...].reshape(1, neurons), v_decay[...].reshape(1, neurons)
    g, v = g_start[...].reshape(1, neurons), v_start[...].reshape(1, neurons)
    scales = [scales_of(r[own_blocks * steps :]) for r in ins]
    for i in range(own_blocks):
        cols = slice(i * width, (i + 1) * width)
        value = inner[i] + own[i]
        for r, scale in zip(ins, scales):
            rows = r[i * steps : (i + 1) * steps].astype(jnp.float32)
            value += rows * scale_of(scale, 0, own_blocks, i)
        current[:, cols] = (1.0 - a[:, cols]) * value
    for t in range(steps):
        g = a * g + current[t : t + 1, :]
        v = b * v + (1.0 - b) * g
        membrane[t : t + 1, :] = v
    g_last[...] = g.reshape(neurons)


def local(
    regions,
    locals_,
    block_flags,
    trace,
    w_region,
    lr_weight,
    lr_source,
    lr_target,
    lr_count,
    g_decay,
    v_decay,
    g_start,
    v_start,
):
    steps = trace.shape[0]
    own_blocks = block_flags.shape[1]
    neurons = trace.shape[1]
    width = neurons // own_blocks
    slots = lr_target.shape[3]
    n_far = locals_ // HALVES
    n_hi = regions // CORES
    per_half = n_far * own_blocks
    f32, i16, bf16, i32 = jnp.float32, jnp.int16, jnp.bfloat16, jnp.int32
    shape = jax.ShapeDtypeStruct
    rows = slots * steps
    pack_rows = rows + steps // 2

    def to(value, k, j):
        pairs = [
            (r * locals_ + l, (r ^ k) * locals_ + (l ^ j))
            for r in range(regions)
            for l in range(locals_)
        ]
        return lax.ppermute(value, ("region", "local"), pairs)

    drive, theirs, *rest = pl.pallas_call(
        functools.partial(first_kernel, per_half),
        out_shape=[
            shape((own_blocks, steps, width), bf16),
            shape((n_hi, pack_rows, width), i16),
            shape((n_hi - 1, slots, width, width), bf16),
            shape((n_hi - 1, slots, steps, width), bf16),
            shape((n_hi - 1, steps // 2, width), i32),
        ],
        in_specs=[HBM] * 6,
        out_specs=[VMEM] * 5,
        scratch_shapes=[
            pltpu.VMEM((own_blocks, steps), i32),
            pltpu.VMEM((steps, neurons), bf16),
            pltpu.SMEM((regions, slots), i32),
            pltpu.SMEM((regions, slots), i32),
            pltpu.SMEM((1, regions), i32),
            pltpu.VMEM((n_hi, slots, width, width), bf16),
            pltpu.VMEM((n_hi, slots, steps, width), bf16),
            pltpu.SemaphoreType.DMA((4 + 2 * n_hi,)),
        ],
        compiler_params=PARAMS,
        name="first_partials",
    )(
        *[
            in_hbm(x)
            for x in (block_flags.T, trace, lr_source[0, 0], lr_target[0, 0], lr_count[0], lr_weight[0, 0])
        ]
    )
    sibling = to(theirs, 1, 0)
    drive_x = to(drive, 0, 1)
    tiles, chosen, meta = rest
    mine, across = pl.pallas_call(
        second_kernel,
        out_shape=[shape((n_hi - 1, pack_rows, width), i16), shape((pack_rows, width), i16)],
        in_specs=[VMEM] * 4,
        out_specs=[VMEM] * 2,
        compiler_params=PARAMS,
        name="second_partials",
    )(chosen, meta, tiles, theirs)
    beside = to(across, 1, 1)
    merged = pl.pallas_call(
        functools.partial(merge_kernel, n_hi - 1, rows),
        out_shape=[shape((2 * rows + steps // 2, width), i16)] * (n_hi - 1),
        in_specs=[VMEM] * 2,
        out_specs=[VMEM] * (n_hi - 1),
        compiler_params=PARAMS,
        name="merge",
    )(sibling, mine)
    pair = pl.pallas_call(
        pair_kernel,
        out_shape=shape((HALVES, own_blocks, steps, width), bf16),
        in_specs=[VMEM] * 2,
        out_specs=VMEM,
        compiler_params=PARAMS,
        cost_estimate=pl.CostEstimate(flops=1 << 36, bytes_accessed=1 << 28, transcendentals=1 << 26),
        name="pair",
    )(drive, drive_x)
    arrived = []
    for k in range(1, n_hi):
        for h in range(HALVES):
            arrived.append(to(merged[k - 1], CORES * k, h))
    drive_order = [2, 3, 1] if n_far == 4 else list(range(1, n_far))
    use_order = [2, 3, 1] if n_far == 4 else list(range(1, n_far))
    sum_order = [2, 3, 1] if n_far == 4 else list(range(1, n_far))
    add_order = [1, 2, 3] if n_far == 4 else list(range(1, n_far))
    pairs = {k: to(pair, 0, k * HALVES) for k in drive_order}

    early = pl.pallas_call(
        functools.partial(early_kernel, slots),
        out_shape=shape((per_half + 1, steps, width), f32),
        in_specs=[VMEM] * 2,
        out_specs=VMEM,
        compiler_params=PARAMS,
        name="add_early",
    )(sibling, beside)
    far_sent = shape((own_blocks * steps + steps // 2, width), i16)
    *sums, own = pl.pallas_call(
        functools.partial(late_kernel, len(arrived), n_far, slots, own_blocks),
        out_shape=[far_sent] * (n_far - 1) + [shape((own_blocks, steps, width), f32)],
        in_specs=[VMEM] * (len(arrived) + 1),
        out_specs=[VMEM] * n_far,
        scratch_shapes=[pltpu.VMEM((per_half + 1, steps, width), f32)],
        compiler_params=PARAMS,
        cost_estimate=pl.CostEstimate(flops=1 << 36, bytes_accessed=1 << 28, transcendentals=1 << 26),
        name="add_late",
    )(early, *arrived)
    far = {k: to(sums[k - 1], 0, k * HALVES) for k in sum_order}

    inner = pl.pallas_call(
        functools.partial(inner_kernel, n_far, (0, *use_order)),
        out_shape=shape((own_blocks, steps, width), f32),
        in_specs=[VMEM] * (n_far + 1),
        out_specs=VMEM,
        compiler_params=PARAMS,
        cost_estimate=pl.CostEstimate(
            flops=2 * steps * neurons * neurons * locals_,
            bytes_accessed=2 * neurons * neurons * locals_,
            transcendentals=0,
        ),
        name="inner",
    )(pair, *[pairs[k] for k in use_order], w_region[0])

    return pl.pallas_call(
        functools.partial(advance_kernel, n_far - 1),
        out_shape=[shape((steps, neurons), f32), shape((neurons,), f32)],
        in_specs=[VMEM] * (n_far + 5),
        out_specs=[VMEM] * 2,
        scratch_shapes=[pltpu.VMEM((steps, neurons), f32)],
        compiler_params=PARAMS,
        name="advance",
    )(inner, own, *[far[k] for k in add_order], g_decay, v_decay, g_start, v_start)


def solution(mesh):
    return jax.shard_map(
        functools.partial(local, mesh.shape["region"], mesh.shape["local"]),
        mesh=mesh,
        in_specs=(
            P(None, ("region", "local")),
            P(None, ("region", "local")),
            P("region", None, "local"),
            P("region", "local", None, None, None, None),
            P("region", "local", None, None),
            P("region", "local", None, None),
            P("region", "local", None),
            P(("region", "local")),
            P(("region", "local")),
            P(("region", "local")),
            P(("region", "local")),
        ),
        out_specs=(P(None, ("region", "local")), P(("region", "local"))),
        check_vma=False,
    )
```

```python
import functools

import jax
import jax.numpy as jnp
from jax import lax
from jax.experimental import pallas as pl
from jax.experimental.pallas import tpu as pltpu
from jax.sharding import PartitionSpec as P

TOP = 32000.0
VMEM = pl.BlockSpec(memory_space=pltpu.VMEM)
HBM = pl.BlockSpec(memory_space=pltpu.HBM)
in_hbm = functools.partial(pltpu.with_memory_space_constraint, memory_space=pltpu.HBM)
PARAMS = pltpu.CompilerParams(vmem_limit_bytes=24 << 20)
CORES = 2
HALVES = 2
SHIFT = 32


def code(value):
    most = jnp.max(jnp.abs(value), axis=-1, keepdims=True)
    power = jnp.ceil(jnp.log2(jnp.maximum(most, 1e-30)) + 1e-5)
    whole = jnp.round(value * (jnp.exp2(-power) * TOP))
    return whole.astype(jnp.int32).astype(jnp.int16), power.astype(jnp.int32)


def put_power(meta, lane, first, count, j, power):
    half = meta.shape[0]
    meta = jnp.where(lane == first + j, power[:half], meta)
    return jnp.where(lane == first + count + j, power[half:], meta)


def scales_of(meta):
    return jnp.exp2(meta.astype(jnp.float32)) * (1.0 / TOP)


def scale_of(scales, first, count, j):
    upper, lower = first + j, first + count + j
    return jnp.concatenate([scales[:, upper : upper + 1], scales[:, lower : lower + 1]], axis=0)


def load_all(pairs, sems):
    copies = [pltpu.make_async_copy(a, b, sems.at[i]) for i, (a, b) in enumerate(pairs)]
    for copy in copies:
        copy.start()
    return copies


def choose(dest, blocks, source, target, count, per_half, first, chosen):
    own_blocks, steps, width = blocks.shape
    slots = source.shape[1]
    lane = lax.broadcasted_iota(jnp.int32, (steps // 2, width), 1)
    live = count[0, dest]
    meta = jnp.zeros((steps // 2, width), jnp.int32)
    for j in range(slots):
        chosen[j] = blocks[source[dest, j]]
        block = target[dest, j]
        owner = (block * (-(-65536 // own_blocks))) >> 16
        place = (owner & (HALVES - 1)) * per_half + (owner >> 1) * own_blocks
        place = jnp.where(j < live, place + block - owner * own_blocks, -1)
        meta = jnp.where(lane == first + 2 * slots + j, place, meta)
    return meta


def send_slots(chosen, tiles, meta, first, out):
    slots, steps, _ = chosen.shape
    lane = lax.broadcasted_iota(jnp.int32, meta.shape, 1)
    for j in range(slots):
        part = jnp.dot(chosen[j], tiles[j], preferred_element_type=jnp.float32)
        whole, power = code(part)
        out[j * steps : (j + 1) * steps] = whole
        meta = put_power(meta, lane, first, slots, j, power)
    out[slots * steps :] = meta.astype(jnp.int16)


def first_kernel(
    per_half,
    flags_h,
    trace_h,
    source_h,
    target_h,
    count_h,
    weight,
    drive,
    out,
    next_tiles,
    next_chosen,
    next_meta,
    flags,
    trace,
    source,
    target,
    count,
    tiles,
    chosen,
    sems,
):
    n = out.shape[0]
    own_blocks, steps, width = drive.shape
    region = lax.axis_index("region")
    copies = load_all(
        [(flags_h, flags), (trace_h, trace), (source_h, source), (target_h, target), (count_h, count)]
        + [(weight.at[region ^ 1 ^ (CORES * k)], tiles.at[k]) for k in range(n)]
        + [(weight.at[region ^ (CORES * (k + 1))], next_tiles.at[k]) for k in range(n - 1)],
        sems,
    )
    for copy in copies[:5]:
        copy.wait()
    row = lax.broadcasted_iota(jnp.int32, (steps, steps), 0)
    col = lax.broadcasted_iota(jnp.int32, (steps, steps), 1)
    for b in range(own_blocks):
        spread = jnp.where(row == col, flags[b : b + 1, :], 0).astype(jnp.float32)
        on = jnp.sum(spread, axis=1, keepdims=True)
        part = trace[:, b * width : (b + 1) * width].astype(jnp.float32)
        drive[b] = (part * on).astype(jnp.bfloat16)
    for k in range(n - 1):
        next_meta[k] = choose(
            region ^ (CORES * (k + 1)), drive, source, target, count, per_half, SHIFT, next_chosen.at[k]
        )
    metas = [
        choose(region ^ 1 ^ (CORES * k), drive, source, target, count, per_half, 0, chosen.at[k])
        for k in range(n)
    ]
    for k in range(n):
        copies[5 + k].wait()
        send_slots(chosen.at[k], tiles.at[k], metas[k], 0, out.at[k])
    for copy in copies[5 + n :]:
        copy.wait()


def second_kernel(chosen, meta, tiles, theirs, out, across):
    across[...] = theirs[0]
    for k in range(out.shape[0]):
        send_slots(chosen.at[k], tiles.at[k], meta[k], SHIFT, out.at[k])


def merge_kernel(n, rows, sibling, mine, *outs):
    for k in range(n):
        outs[k][:rows] = mine[k, :rows]
        outs[k][rows : 2 * rows] = sibling[k + 1, :rows]
        meta = mine[k, rows:].astype(jnp.int32) + sibling[k + 1, rows:].astype(jnp.int32)
        outs[k][2 * rows :] = meta.astype(jnp.int16)


def pair_kernel(drive, drive_x, pair):
    half = lax.axis_index("local") % HALVES
    pair[half] = drive[...]
    pair[1 - half] = drive_x[...]


def add_packs(packs, slots, steps, per_half, total):
    half = lax.axis_index("local") % HALVES
    for ref, row, meta, first in packs:
        block = ref[meta : meta + steps // 2]
        scales = scales_of(block)
        line = block.astype(jnp.int32)[0:1]
        for j in range(slots):
            place = line[0, first + 2 * slots + j] - half * per_half
            place = jnp.where((place >= 0) & (place < per_half), place, per_half)
            rows = ref[row + j * steps : row + (j + 1) * steps].astype(jnp.float32)
            total[place] += rows * scale_of(scales, first, slots, j)


def early_kernel(slots, sibling, beside, total):
    steps = total.shape[1]
    total[...] = jnp.zeros_like(total)
    packs = [(sibling.at[0], 0, slots * steps, 0), (beside, 0, slots * steps, 0)]
    add_packs(packs, slots, steps, total.shape[0] - 1, total)


def late_kernel(n_in, n_far, slots, own_blocks, early, *refs):
    ins = refs[:n_in]
    outs = refs[n_in : n_in + n_far - 1]
    own, total = refs[n_in + n_far - 1 :]
    steps, width = total.shape[1:]
    far = lax.axis_index("local") // HALVES
    total[...] = early[...]
    packs = []
    for r in ins:
        packs += [(r, 0, 2 * slots * steps, SHIFT), (r, slots * steps, 2 * slots * steps, 0)]
    add_packs(packs, slots, steps, n_far * own_blocks, total)
    lane = lax.broadcasted_iota(jnp.int32, (steps // 2, width), 1)
    for i in range(own_blocks):
        own[i] = total[far * own_blocks + i]
    for k in range(1, n_far):
        meta = jnp.zeros((steps // 2, width), jnp.int32)
        for i in range(own_blocks):
            whole, power = code(total[(far ^ k) * own_blocks + i])
            outs[k - 1][i * steps : (i + 1) * steps] = whole
            meta = put_power(meta, lane, 0, own_blocks, i, power)
        outs[k - 1][own_blocks * steps :] = meta.astype(jnp.int16)


def inner_kernel(n_far, order, *refs):
    pairs = refs[:n_far]
    weight, out = refs[n_far:]
    halves, own_blocks, steps, width = pairs[0].shape
    depth = own_blocks * width
    far = lax.axis_index("local") // HALVES
    total = jnp.zeros((steps, depth), jnp.float32)
    for k in range(n_far):
        left = jnp.concatenate(
            [pairs[k][h, b] for h in range(halves) for b in range(own_blocks)], axis=1
        )
        rows = pl.ds(pl.multiple_of((far ^ order[k]) * halves * depth, halves * depth), halves * depth)
        total += jnp.dot(left, weight[rows, :], preferred_element_type=jnp.float32)
    for b in range(own_blocks):
        out[b] = total[:, b * width : (b + 1) * width]


def advance_kernel(n_in, inner, own, *refs):
    ins = refs[:n_in]
    g_decay, v_decay, g_start, v_start, membrane, g_last, current = refs[n_in:]
    own_blocks, steps, width = own.shape
    neurons = own_blocks * width
    a, b = g_decay[...].reshape(1, neurons), v_decay[...].reshape(1, neurons)
    g, v = g_start[...].reshape(1, neurons), v_start[...].reshape(1, neurons)
    scales = [scales_of(r[own_blocks * steps :]) for r in ins]
    for i in range(own_blocks):
        cols = slice(i * width, (i + 1) * width)
        value = inner[i] + own[i]
        for r, scale in zip(ins, scales):
            rows = r[i * steps : (i + 1) * steps].astype(jnp.float32)
            value += rows * scale_of(scale, 0, own_blocks, i)
        current[:, cols] = (1.0 - a[:, cols]) * value
    for t in range(steps):
        g = a * g + current[t : t + 1, :]
        v = b * v + (1.0 - b) * g
        membrane[t : t + 1, :] = v
    g_last[...] = g.reshape(neurons)


def local(
    regions,
    locals_,
    block_flags,
    trace,
    w_region,
    lr_weight,
    lr_source,
    lr_target,
    lr_count,
    g_decay,
    v_decay,
    g_start,
    v_start,
):
    steps = trace.shape[0]
    own_blocks = block_flags.shape[1]
    neurons = trace.shape[1]
    width = neurons // own_blocks
    slots = lr_target.shape[3]
    n_far = locals_ // HALVES
    n_hi = regions // CORES
    per_half = n_far * own_blocks
    f32, i16, bf16, i32 = jnp.float32, jnp.int16, jnp.bfloat16, jnp.int32
    shape = jax.ShapeDtypeStruct
    rows = slots * steps
    pack_rows = rows + steps // 2

    def to(value, k, j):
        pairs = [
            (r * locals_ + l, (r ^ k) * locals_ + (l ^ j))
            for r in range(regions)
            for l in range(locals_)
        ]
        return lax.ppermute(value, ("region", "local"), pairs)

    drive, theirs, *rest = pl.pallas_call(
        functools.partial(first_kernel, per_half),
        out_shape=[
            shape((own_blocks, steps, width), bf16),
            shape((n_hi, pack_rows, width), i16),
            shape((n_hi - 1, slots, width, width), bf16),
            shape((n_hi - 1, slots, steps, width), bf16),
            shape((n_hi - 1, steps // 2, width), i32),
        ],
        in_specs=[HBM] * 6,
        out_specs=[VMEM] * 5,
        scratch_shapes=[
            pltpu.VMEM((own_blocks, steps), i32),
            pltpu.VMEM((steps, neurons), bf16),
            pltpu.SMEM((regions, slots), i32),
            pltpu.SMEM((regions, slots), i32),
            pltpu.SMEM((1, regions), i32),
            pltpu.VMEM((n_hi, slots, width, width), bf16),
            pltpu.VMEM((n_hi, slots, steps, width), bf16),
            pltpu.SemaphoreType.DMA((4 + 2 * n_hi,)),
        ],
        compiler_params=PARAMS,
        name="first_partials",
    )(
        *[
            in_hbm(x)
            for x in (block_flags.T, trace, lr_source[0, 0], lr_target[0, 0], lr_count[0], lr_weight[0, 0])
        ]
    )
    sibling = to(theirs, 1, 0)
    drive_x = to(drive, 0, 1)
    tiles, chosen, meta = rest
    mine, across = pl.pallas_call(
        second_kernel,
        out_shape=[shape((n_hi - 1, pack_rows, width), i16), shape((pack_rows, width), i16)],
        in_specs=[VMEM] * 4,
        out_specs=[VMEM] * 2,
        compiler_params=PARAMS,
        name="second_partials",
    )(chosen, meta, tiles, theirs)
    beside = to(across, 1, 1)
    merged = pl.pallas_call(
        functools.partial(merge_kernel, n_hi - 1, rows),
        out_shape=[shape((2 * rows + steps // 2, width), i16)] * (n_hi - 1),
        in_specs=[VMEM] * 2,
        out_specs=[VMEM] * (n_hi - 1),
        compiler_params=PARAMS,
        name="merge",
    )(sibling, mine)
    pair = pl.pallas_call(
        pair_kernel,
        out_shape=shape((HALVES, own_blocks, steps, width), bf16),
        in_specs=[VMEM] * 2,
        out_specs=VMEM,
        compiler_params=PARAMS,
        cost_estimate=pl.CostEstimate(flops=1 << 36, bytes_accessed=1 << 28, transcendentals=1 << 26),
        name="pair",
    )(drive, drive_x)
    arrived = []
    for k in range(1, n_hi):
        for h in range(HALVES):
            arrived.append(to(merged[k - 1], CORES * k, h))
    drive_order = [2, 3, 1] if n_far == 4 else list(range(1, n_far))
    use_order = [2, 1, 3] if n_far == 4 else list(range(1, n_far))
    sum_order = [2, 3, 1] if n_far == 4 else list(range(1, n_far))
    add_order = [1, 2, 3] if n_far == 4 else list(range(1, n_far))
    pairs = {k: to(pair, 0, k * HALVES) for k in drive_order}

    early = pl.pallas_call(
        functools.partial(early_kernel, slots),
        out_shape=shape((per_half + 1, steps, width), f32),
        in_specs=[VMEM] * 2,
        out_specs=VMEM,
        compiler_params=PARAMS,
        name="add_early",
    )(sibling, beside)
    far_sent = shape((own_blocks * steps + steps // 2, width), i16)
    *sums, own = pl.pallas_call(
        functools.partial(late_kernel, len(arrived), n_far, slots, own_blocks),
        out_shape=[far_sent] * (n_far - 1) + [shape((own_blocks, steps, width), f32)],
        in_specs=[VMEM] * (len(arrived) + 1),
        out_specs=[VMEM] * n_far,
        scratch_shapes=[pltpu.VMEM((per_half + 1, steps, width), f32)],
        compiler_params=PARAMS,
        cost_estimate=pl.CostEstimate(flops=1 << 36, bytes_accessed=1 << 28, transcendentals=1 << 26),
        name="add_late",
    )(early, *arrived)
    far = {k: to(sums[k - 1], 0, k * HALVES) for k in sum_order}

    inner = pl.pallas_call(
        functools.partial(inner_kernel, n_far, (0, *use_order)),
        out_shape=shape((own_blocks, steps, width), f32),
        in_specs=[VMEM] * (n_far + 1),
        out_specs=VMEM,
        compiler_params=PARAMS,
        cost_estimate=pl.CostEstimate(
            flops=2 * steps * neurons * neurons * locals_,
            bytes_accessed=2 * neurons * neurons * locals_,
            transcendentals=0,
        ),
        name="inner",
    )(pair, *[pairs[k] for k in use_order], w_region[0])

    return pl.pallas_call(
        functools.partial(advance_kernel, n_far - 1),
        out_shape=[shape((steps, neurons), f32), shape((neurons,), f32)],
        in_specs=[VMEM] * (n_far + 5),
        out_specs=[VMEM] * 2,
        scratch_shapes=[pltpu.VMEM((steps, neurons), f32)],
        compiler_params=PARAMS,
        name="advance",
    )(inner, own, *[far[k] for k in add_order], g_decay, v_decay, g_start, v_start)


def solution(mesh):
    return jax.shard_map(
        functools.partial(local, mesh.shape["region"], mesh.shape["local"]),
        mesh=mesh,
        in_specs=(
            P(None, ("region", "local")),
            P(None, ("region", "local")),
            P("region", None, "local"),
            P("region", "local", None, None, None, None),
            P("region", "local", None, None),
            P("region", "local", None, None),
            P("region", "local", None),
            P(("region", "local")),
            P(("region", "local")),
            P(("region", "local")),
            P(("region", "local")),
        ),
        out_specs=(P(None, ("region", "local")), P(("region", "local"))),
        check_vma=False,
    )
```

```python
import functools

import jax
import jax.numpy as jnp
from jax import lax
from jax.experimental import pallas as pl
from jax.experimental.pallas import tpu as pltpu
from jax.sharding import PartitionSpec as P

TOP = 32000.0
VMEM = pl.BlockSpec(memory_space=pltpu.VMEM)
HBM = pl.BlockSpec(memory_space=pltpu.HBM)
in_hbm = functools.partial(pltpu.with_memory_space_constraint, memory_space=pltpu.HBM)
PARAMS = pltpu.CompilerParams(vmem_limit_bytes=24 << 20)
CORES = 2
HALVES = 2
SHIFT = 32


def code(value):
    most = jnp.max(jnp.abs(value), axis=-1, keepdims=True)
    power = jnp.ceil(jnp.log2(jnp.maximum(most, 1e-30)) + 1e-5)
    whole = jnp.round(value * (jnp.exp2(-power) * TOP))
    return whole.astype(jnp.int32).astype(jnp.int16), power.astype(jnp.int32)


def put_power(meta, lane, first, count, j, power):
    half = meta.shape[0]
    meta = jnp.where(lane == first + j, power[:half], meta)
    return jnp.where(lane == first + count + j, power[half:], meta)


def scales_of(meta):
    return jnp.exp2(meta.astype(jnp.float32)) * (1.0 / TOP)


def scale_of(scales, first, count, j):
    upper, lower = first + j, first + count + j
    return jnp.concatenate([scales[:, upper : upper + 1], scales[:, lower : lower + 1]], axis=0)


def load_all(pairs, sems):
    copies = [pltpu.make_async_copy(a, b, sems.at[i]) for i, (a, b) in enumerate(pairs)]
    for copy in copies:
        copy.start()
    return copies


def choose(dest, blocks, source, target, count, per_half, first, chosen):
    own_blocks, steps, width = blocks.shape
    slots = source.shape[1]
    lane = lax.broadcasted_iota(jnp.int32, (steps // 2, width), 1)
    live = count[0, dest]
    meta = jnp.zeros((steps // 2, width), jnp.int32)
    for j in range(slots):
        chosen[j] = blocks[source[dest, j]]
        block = target[dest, j]
        owner = (block * (-(-65536 // own_blocks))) >> 16
        place = (owner & (HALVES - 1)) * per_half + (owner >> 1) * own_blocks
        place = jnp.where(j < live, place + block - owner * own_blocks, -1)
        meta = jnp.where(lane == first + 2 * slots + j, place, meta)
    return meta


def send_slots(chosen, tiles, meta, first, out):
    slots, steps, _ = chosen.shape
    lane = lax.broadcasted_iota(jnp.int32, meta.shape, 1)
    for j in range(slots):
        part = jnp.dot(chosen[j], tiles[j], preferred_element_type=jnp.float32)
        whole, power = code(part)
        out[j * steps : (j + 1) * steps] = whole
        meta = put_power(meta, lane, first, slots, j, power)
    out[slots * steps :] = meta.astype(jnp.int16)


def first_kernel(
    per_half,
    flags_h,
    trace_h,
    source_h,
    target_h,
    count_h,
    weight,
    drive,
    out,
    next_tiles,
    next_chosen,
    next_meta,
    flags,
    trace,
    source,
    target,
    count,
    tiles,
    chosen,
    sems,
):
    n = out.shape[0]
    own_blocks, steps, width = drive.shape
    region = lax.axis_index("region")
    copies = load_all(
        [(flags_h, flags), (trace_h, trace), (source_h, source), (target_h, target), (count_h, count)]
        + [(weight.at[region ^ 1 ^ (CORES * k)], tiles.at[k]) for k in range(n)]
        + [(weight.at[region ^ (CORES * (k + 1))], next_tiles.at[k]) for k in range(n - 1)],
        sems,
    )
    for copy in copies[:5]:
        copy.wait()
    row = lax.broadcasted_iota(jnp.int32, (steps, steps), 0)
    col = lax.broadcasted_iota(jnp.int32, (steps, steps), 1)
    for b in range(own_blocks):
        spread = jnp.where(row == col, flags[b : b + 1, :], 0).astype(jnp.float32)
        on = jnp.sum(spread, axis=1, keepdims=True)
        part = trace[:, b * width : (b + 1) * width].astype(jnp.float32)
        drive[b] = (part * on).astype(jnp.bfloat16)
    for k in range(n - 1):
        next_meta[k] = choose(
            region ^ (CORES * (k + 1)), drive, source, target, count, per_half, SHIFT, next_chosen.at[k]
        )
    metas = [
        choose(region ^ 1 ^ (CORES * k), drive, source, target, count, per_half, 0, chosen.at[k])
        for k in range(n)
    ]
    for copy in copies[5:]:
        copy.wait()
    for k in range(n):
        send_slots(chosen.at[k], tiles.at[k], metas[k], 0, out.at[k])


def second_kernel(chosen, meta, tiles, theirs, out, across):
    across[...] = theirs[0]
    for k in range(out.shape[0]):
        send_slots(chosen.at[k], tiles.at[k], meta[k], SHIFT, out.at[k])


def merge_kernel(n, rows, sibling, mine, *outs):
    for k in range(n):
        outs[k][:rows] = mine[k, :rows]
        outs[k][rows : 2 * rows] = sibling[k + 1, :rows]
        meta = mine[k, rows:].astype(jnp.int32) + sibling[k + 1, rows:].astype(jnp.int32)
        outs[k][2 * rows :] = meta.astype(jnp.int16)


def pair_kernel(drive, drive_x, pair):
    half = lax.axis_index("local") % HALVES
    pair[half] = drive[...]
    pair[1 - half] = drive_x[...]


def add_packs(packs, slots, steps, per_half, total):
    half = lax.axis_index("local") % HALVES
    for ref, row, meta, first in packs:
        block = ref[meta : meta + steps // 2]
        scales = scales_of(block)
        line = block.astype(jnp.int32)[0:1]
        for j in range(slots):
            place = line[0, first + 2 * slots + j] - half * per_half
            place = jnp.where((place >= 0) & (place < per_half), place, per_half)
            rows = ref[row + j * steps : row + (j + 1) * steps].astype(jnp.float32)
            total[place] += rows * scale_of(scales, first, slots, j)


def early_kernel(slots, sibling, beside, total):
    steps = total.shape[1]
    total[...] = jnp.zeros_like(total)
    packs = [(sibling.at[0], 0, slots * steps, 0), (beside, 0, slots * steps, 0)]
    add_packs(packs, slots, steps, total.shape[0] - 1, total)


def late_kernel(n_in, n_far, slots, own_blocks, early, *refs):
    ins = refs[:n_in]
    outs = refs[n_in : n_in + n_far - 1]
    own, total = refs[n_in + n_far - 1 :]
    steps, width = total.shape[1:]
    far = lax.axis_index("local") // HALVES
    total[...] = early[...]
    packs = []
    for r in ins:
        packs += [(r, 0, 2 * slots * steps, SHIFT), (r, slots * steps, 2 * slots * steps, 0)]
    add_packs(packs, slots, steps, n_far * own_blocks, total)
    lane = lax.broadcasted_iota(jnp.int32, (steps // 2, width), 1)
    for i in range(own_blocks):
        own[i] = total[far * own_blocks + i]
    for k in range(1, n_far):
        meta = jnp.zeros((steps // 2, width), jnp.int32)
        for i in range(own_blocks):
            whole, power = code(total[(far ^ k) * own_blocks + i])
            outs[k - 1][i * steps : (i + 1) * steps] = whole
            meta = put_power(meta, lane, 0, own_blocks, i, power)
        outs[k - 1][own_blocks * steps :] = meta.astype(jnp.int16)


def inner_kernel(n_far, order, *refs):
    pairs = refs[:n_far]
    weight, out = refs[n_far:]
    halves, own_blocks, steps, width = pairs[0].shape
    depth = own_blocks * width
    far = lax.axis_index("local") // HALVES
    total = jnp.zeros((steps, depth), jnp.float32)
    for k in range(n_far):
        left = jnp.concatenate(
            [pairs[k][h, b] for h in range(halves) for b in range(own_blocks)], axis=1
        )
        rows = pl.ds(pl.multiple_of((far ^ order[k]) * halves * depth, halves * depth), halves * depth)
        total += jnp.dot(left, weight[rows, :], preferred_element_type=jnp.float32)
    for b in range(own_blocks):
        out[b] = total[:, b * width : (b + 1) * width]


def advance_kernel(n_in, inner, own, *refs):
    ins = refs[:n_in]
    g_decay, v_decay, g_start, v_start, membrane, g_last, current = refs[n_in:]
    own_blocks, steps, width = own.shape
    neurons = own_blocks * width
    a, b = g_decay[...].reshape(1, neurons), v_decay[...].reshape(1, neurons)
    g, v = g_start[...].reshape(1, neurons), v_start[...].reshape(1, neurons)
    scales = [scales_of(r[own_blocks * steps :]) for r in ins]
    for i in range(own_blocks):
        cols = slice(i * width, (i + 1) * width)
        value = inner[i] + own[i]
        for r, scale in zip(ins, scales):
            rows = r[i * steps : (i + 1) * steps].astype(jnp.float32)
            value += rows * scale_of(scale, 0, own_blocks, i)
        current[:, cols] = (1.0 - a[:, cols]) * value
    for t in range(steps):
        g = a * g + current[t : t + 1, :]
        v = b * v + (1.0 - b) * g
        membrane[t : t + 1, :] = v
    g_last[...] = g.reshape(neurons)


def local(
    regions,
    locals_,
    block_flags,
    trace,
    w_region,
    lr_weight,
    lr_source,
    lr_target,
    lr_count,
    g_decay,
    v_decay,
    g_start,
    v_start,
):
    steps = trace.shape[0]
    own_blocks = block_flags.shape[1]
    neurons = trace.shape[1]
    width = neurons // own_blocks
    slots = lr_target.shape[3]
    n_far = locals_ // HALVES
    n_hi = regions // CORES
    per_half = n_far * own_blocks
    f32, i16, bf16, i32 = jnp.float32, jnp.int16, jnp.bfloat16, jnp.int32
    shape = jax.ShapeDtypeStruct
    rows = slots * steps
    pack_rows = rows + steps // 2

    def to(value, k, j):
        pairs = [
            (r * locals_ + l, (r ^ k) * locals_ + (l ^ j))
            for r in range(regions)
            for l in range(locals_)
        ]
        return lax.ppermute(value, ("region", "local"), pairs)

    drive, theirs, *rest = pl.pallas_call(
        functools.partial(first_kernel, per_half),
        out_shape=[
            shape((own_blocks, steps, width), bf16),
            shape((n_hi, pack_rows, width), i16),
            shape((n_hi - 1, slots, width, width), bf16),
            shape((n_hi - 1, slots, steps, width), bf16),
            shape((n_hi - 1, steps // 2, width), i32),
        ],
        in_specs=[HBM] * 6,
        out_specs=[VMEM] * 5,
        scratch_shapes=[
            pltpu.VMEM((own_blocks, steps), i32),
            pltpu.VMEM((steps, neurons), bf16),
            pltpu.SMEM((regions, slots), i32),
            pltpu.SMEM((regions, slots), i32),
            pltpu.SMEM((1, regions), i32),
            pltpu.VMEM((n_hi, slots, width, width), bf16),
            pltpu.VMEM((n_hi, slots, steps, width), bf16),
            pltpu.SemaphoreType.DMA((4 + 2 * n_hi,)),
        ],
        compiler_params=PARAMS,
        name="first_partials",
    )(
        *[
            in_hbm(x)
            for x in (block_flags.T, trace, lr_source[0, 0], lr_target[0, 0], lr_count[0], lr_weight[0, 0])
        ]
    )
    sibling = to(theirs, 1, 0)
    drive_x = to(drive, 0, 1)
    tiles, chosen, meta = rest
    mine, across = pl.pallas_call(
        second_kernel,
        out_shape=[shape((n_hi - 1, pack_rows, width), i16), shape((pack_rows, width), i16)],
        in_specs=[VMEM] * 4,
        out_specs=[VMEM] * 2,
        compiler_params=PARAMS,
        name="second_partials",
    )(chosen, meta, tiles, theirs)
    beside = to(across, 1, 1)
    merged = pl.pallas_call(
        functools.partial(merge_kernel, n_hi - 1, rows),
        out_shape=[shape((2 * rows + steps // 2, width), i16)] * (n_hi - 1),
        in_specs=[VMEM] * 2,
        out_specs=[VMEM] * (n_hi - 1),
        compiler_params=PARAMS,
        name="merge",
    )(sibling, mine)
    pair = pl.pallas_call(
        pair_kernel,
        out_shape=shape((HALVES, own_blocks, steps, width), bf16),
        in_specs=[VMEM] * 2,
        out_specs=VMEM,
        compiler_params=PARAMS,
        cost_estimate=pl.CostEstimate(flops=1 << 36, bytes_accessed=1 << 28, transcendentals=1 << 26),
        name="pair",
    )(drive, drive_x)
    arrived = []
    for k in range(1, n_hi):
        for h in range(HALVES):
            arrived.append(to(merged[k - 1], CORES * k, h))
    drive_order = [2, 3, 1] if n_far == 4 else list(range(1, n_far))
    use_order = [2, 1, 3] if n_far == 4 else list(range(1, n_far))
    sum_order = [2, 3, 1] if n_far == 4 else list(range(1, n_far))
    add_order = [1, 2, 3] if n_far == 4 else list(range(1, n_far))
    pairs = {k: to(pair, 0, k * HALVES) for k in drive_order}

    early = pl.pallas_call(
        functools.partial(early_kernel, slots),
        out_shape=shape((per_half + 1, steps, width), f32),
        in_specs=[VMEM] * 2,
        out_specs=VMEM,
        compiler_params=PARAMS,
        name="add_early",
    )(sibling, beside)
    far_sent = shape((own_blocks * steps + steps // 2, width), i16)
    *sums, own = pl.pallas_call(
        functools.partial(late_kernel, len(arrived), n_far, slots, own_blocks),
        out_shape=[far_sent] * (n_far - 1) + [shape((own_blocks, steps, width), f32)],
        in_specs=[VMEM] * (len(arrived) + 1),
        out_specs=[VMEM] * n_far,
        scratch_shapes=[pltpu.VMEM((per_half + 1, steps, width), f32)],
        compiler_params=PARAMS,
        cost_estimate=pl.CostEstimate(flops=1 << 36, bytes_accessed=1 << 28, transcendentals=1 << 26),
        name="add_late",
    )(early, *arrived)
    far = {k: to(sums[k - 1], 0, k * HALVES) for k in sum_order}

    inner = pl.pallas_call(
        functools.partial(inner_kernel, n_far, (0, *use_order)),
        out_shape=shape((own_blocks, steps, width), f32),
        in_specs=[VMEM] * (n_far + 1),
        out_specs=VMEM,
        compiler_params=PARAMS,
        cost_estimate=pl.CostEstimate(
            flops=2 * steps * neurons * neurons * locals_,
            bytes_accessed=2 * neurons * neurons * locals_,
            transcendentals=0,
        ),
        name="inner",
    )(pair, *[pairs[k] for k in use_order], w_region[0])

    return pl.pallas_call(
        functools.partial(advance_kernel, n_far - 1),
        out_shape=[shape((steps, neurons), f32), shape((neurons,), f32)],
        in_specs=[VMEM] * (n_far + 5),
        out_specs=[VMEM] * 2,
        scratch_shapes=[pltpu.VMEM((steps, neurons), f32)],
        compiler_params=PARAMS,
        name="advance",
    )(inner, own, *[far[k] for k in add_order], g_decay, v_decay, g_start, v_start)


def solution(mesh):
    return jax.shard_map(
        functools.partial(local, mesh.shape["region"], mesh.shape["local"]),
        mesh=mesh,
        in_specs=(
            P(None, ("region", "local")),
            P(None, ("region", "local")),
            P("region", None, "local"),
            P("region", "local", None, None, None, None),
            P("region", "local", None, None),
            P("region", "local", None, None),
            P("region", "local", None),
            P(("region", "local")),
            P(("region", "local")),
            P(("region", "local")),
            P(("region", "local")),
        ),
        out_specs=(P(None, ("region", "local")), P(("region", "local"))),
        check_vma=False,
    )
```

```python
import functools

import jax
import jax.numpy as jnp
from jax import lax
from jax.experimental import pallas as pl
from jax.experimental.pallas import tpu as pltpu
from jax.sharding import PartitionSpec as P

TOP = 32000.0
VMEM = pl.BlockSpec(memory_space=pltpu.VMEM)
HBM = pl.BlockSpec(memory_space=pltpu.HBM)
in_hbm = functools.partial(pltpu.with_memory_space_constraint, memory_space=pltpu.HBM)
PARAMS = pltpu.CompilerParams(vmem_limit_bytes=24 << 20)
CORES = 2
HALVES = 2
SHIFT = 32


def code(value):
    most = jnp.max(jnp.abs(value), axis=-1, keepdims=True)
    power = jnp.ceil(jnp.log2(jnp.maximum(most, 1e-30)) + 1e-5)
    whole = jnp.round(value * (jnp.exp2(-power) * TOP))
    return whole.astype(jnp.int32).astype(jnp.int16), power.astype(jnp.int32)


def put_power(meta, lane, first, count, j, power):
    half = meta.shape[0]
    meta = jnp.where(lane == first + j, power[:half], meta)
    return jnp.where(lane == first + count + j, power[half:], meta)


def scales_of(meta):
    return jnp.exp2(meta.astype(jnp.float32)) * (1.0 / TOP)


def scale_of(scales, first, count, j):
    upper, lower = first + j, first + count + j
    return jnp.concatenate([scales[:, upper : upper + 1], scales[:, lower : lower + 1]], axis=0)


def load_all(pairs, sems):
    copies = [pltpu.make_async_copy(a, b, sems.at[i]) for i, (a, b) in enumerate(pairs)]
    for copy in copies:
        copy.start()
    return copies


def choose(dest, blocks, source, target, count, per_half, first, chosen):
    own_blocks, steps, width = blocks.shape
    slots = source.shape[1]
    lane = lax.broadcasted_iota(jnp.int32, (steps // 2, width), 1)
    live = count[0, dest]
    meta = jnp.zeros((steps // 2, width), jnp.int32)
    for j in range(slots):
        chosen[j] = blocks[source[dest, j]]
        block = target[dest, j]
        owner = (block * (-(-65536 // own_blocks))) >> 16
        place = (owner & (HALVES - 1)) * per_half + (owner >> 1) * own_blocks
        place = jnp.where(j < live, place + block - owner * own_blocks, -1)
        meta = jnp.where(lane == first + 2 * slots + j, place, meta)
    return meta


def send_slots(chosen, tiles, meta, first, out):
    slots, steps, _ = chosen.shape
    lane = lax.broadcasted_iota(jnp.int32, meta.shape, 1)
    for j in range(slots):
        part = jnp.dot(chosen[j], tiles[j], preferred_element_type=jnp.float32)
        whole, power = code(part)
        out[j * steps : (j + 1) * steps] = whole
        meta = put_power(meta, lane, first, slots, j, power)
    out[slots * steps :] = meta.astype(jnp.int16)


def first_kernel(
    per_half,
    flags_h,
    trace_h,
    source_h,
    target_h,
    count_h,
    weight,
    drive,
    out,
    next_tiles,
    next_chosen,
    next_meta,
    flags,
    trace,
    source,
    target,
    count,
    tiles,
    chosen,
    sems,
):
    n = out.shape[0]
    own_blocks, steps, width = drive.shape
    region = lax.axis_index("region")
    copies = load_all(
        [(flags_h, flags), (trace_h, trace), (source_h, source), (target_h, target), (count_h, count)]
        + [(weight.at[region ^ 1 ^ (CORES * k)], tiles.at[k]) for k in range(n)]
        + [(weight.at[region ^ (CORES * (k + 1))], next_tiles.at[k]) for k in range(n - 1)],
        sems,
    )
    for copy in copies[:5]:
        copy.wait()
    row = lax.broadcasted_iota(jnp.int32, (steps, steps), 0)
    col = lax.broadcasted_iota(jnp.int32, (steps, steps), 1)
    for b in range(own_blocks):
        spread = jnp.where(row == col, flags[b : b + 1, :], 0).astype(jnp.float32)
        on = jnp.sum(spread, axis=1, keepdims=True)
        part = trace[:, b * width : (b + 1) * width].astype(jnp.float32)
        drive[b] = (part * on).astype(jnp.bfloat16)
    for k in range(n - 1):
        next_meta[k] = choose(
            region ^ (CORES * (k + 1)), drive, source, target, count, per_half, SHIFT, next_chosen.at[k]
        )
    metas = [
        choose(region ^ 1 ^ (CORES * k), drive, source, target, count, per_half, 0, chosen.at[k])
        for k in range(n)
    ]
    for copy in copies[5:]:
        copy.wait()
    for k in range(n):
        send_slots(chosen.at[k], tiles.at[k], metas[k], 0, out.at[k])


def second_kernel(chosen, meta, tiles, theirs, out, across):
    across[...] = theirs[0]
    for k in range(out.shape[0]):
        send_slots(chosen.at[k], tiles.at[k], meta[k], SHIFT, out.at[k])


def merge_kernel(n, rows, sibling, mine, *outs):
    for k in range(n):
        outs[k][:rows] = mine[k, :rows]
        outs[k][rows : 2 * rows] = sibling[k + 1, :rows]
        meta = mine[k, rows:].astype(jnp.int32) + sibling[k + 1, rows:].astype(jnp.int32)
        outs[k][2 * rows :] = meta.astype(jnp.int16)


def pair_kernel(drive, drive_x, pair):
    half = lax.axis_index("local") % HALVES
    pair[half] = drive[...]
    pair[1 - half] = drive_x[...]


def add_packs(packs, slots, steps, per_half, total):
    half = lax.axis_index("local") % HALVES
    for ref, row, meta, first in packs:
        block = ref[meta : meta + steps // 2]
        scales = scales_of(block)
        line = block.astype(jnp.int32)[0:1]
        for j in range(slots):
            place = line[0, first + 2 * slots + j] - half * per_half
            place = jnp.where((place >= 0) & (place < per_half), place, per_half)
            rows = ref[row + j * steps : row + (j + 1) * steps].astype(jnp.float32)
            total[place] += rows * scale_of(scales, first, slots, j)


def early_kernel(slots, sibling, beside, total):
    steps = total.shape[1]
    total[...] = jnp.zeros_like(total)
    packs = [(sibling.at[0], 0, slots * steps, 0), (beside, 0, slots * steps, 0)]
    add_packs(packs, slots, steps, total.shape[0] - 1, total)


def late_kernel(n_in, n_far, slots, own_blocks, early, *refs):
    ins = refs[:n_in]
    outs = refs[n_in : n_in + n_far - 1]
    own, total = refs[n_in + n_far - 1 :]
    steps, width = total.shape[1:]
    far = lax.axis_index("local") // HALVES
    total[...] = early[...]
    packs = []
    for r in ins:
        packs += [(r, 0, 2 * slots * steps, SHIFT), (r, slots * steps, 2 * slots * steps, 0)]
    add_packs(packs, slots, steps, n_far * own_blocks, total)
    lane = lax.broadcasted_iota(jnp.int32, (steps // 2, width), 1)
    for i in range(own_blocks):
        own[i] = total[far * own_blocks + i]
    for k in range(1, n_far):
        meta = jnp.zeros((steps // 2, width), jnp.int32)
        for i in range(own_blocks):
            whole, power = code(total[(far ^ k) * own_blocks + i])
            outs[k - 1][i * steps : (i + 1) * steps] = whole
            meta = put_power(meta, lane, 0, own_blocks, i, power)
        outs[k - 1][own_blocks * steps :] = meta.astype(jnp.int16)


def inner_kernel(n_far, order, *refs):
    pairs = refs[:n_far]
    weight, out = refs[n_far:]
    halves, own_blocks, steps, width = pairs[0].shape
    depth = own_blocks * width
    far = lax.axis_index("local") // HALVES
    total = jnp.zeros((steps, depth), jnp.float32)
    for k in range(n_far):
        left = jnp.concatenate(
            [pairs[k][h, b] for h in range(halves) for b in range(own_blocks)], axis=1
        )
        rows = pl.ds(pl.multiple_of((far ^ order[k]) * halves * depth, halves * depth), halves * depth)
        total += jnp.dot(left, weight[rows, :], preferred_element_type=jnp.float32)
    for b in range(own_blocks):
        out[b] = total[:, b * width : (b + 1) * width]


def advance_kernel(n_in, inner, own, *refs):
    ins = refs[:n_in]
    g_decay, v_decay, g_start, v_start, membrane, g_last, current = refs[n_in:]
    own_blocks, steps, width = own.shape
    neurons = own_blocks * width
    a, b = g_decay[...].reshape(1, neurons), v_decay[...].reshape(1, neurons)
    g, v = g_start[...].reshape(1, neurons), v_start[...].reshape(1, neurons)
    scales = [scales_of(r[own_blocks * steps :]) for r in ins]
    for i in range(own_blocks):
        cols = slice(i * width, (i + 1) * width)
        value = inner[i] + own[i]
        for r, scale in zip(ins, scales):
            rows = r[i * steps : (i + 1) * steps].astype(jnp.float32)
            value += rows * scale_of(scale, 0, own_blocks, i)
        current[:, cols] = (1.0 - a[:, cols]) * value
    for t in range(steps):
        g = a * g + current[t : t + 1, :]
        v = b * v + (1.0 - b) * g
        membrane[t : t + 1, :] = v
    g_last[...] = g.reshape(neurons)


def local(
    regions,
    locals_,
    block_flags,
    trace,
    w_region,
    lr_weight,
    lr_source,
    lr_target,
    lr_count,
    g_decay,
    v_decay,
    g_start,
    v_start,
):
    steps = trace.shape[0]
    own_blocks = block_flags.shape[1]
    neurons = trace.shape[1]
    width = neurons // own_blocks
    slots = lr_target.shape[3]
    n_far = locals_ // HALVES
    n_hi = regions // CORES
    per_half = n_far * own_blocks
    f32, i16, bf16, i32 = jnp.float32, jnp.int16, jnp.bfloat16, jnp.int32
    shape = jax.ShapeDtypeStruct
    rows = slots * steps
    pack_rows = rows + steps // 2

    def to(value, k, j):
        pairs = [
            (r * locals_ + l, (r ^ k) * locals_ + (l ^ j))
            for r in range(regions)
            for l in range(locals_)
        ]
        return lax.ppermute(value, ("region", "local"), pairs)

    drive, theirs, *rest = pl.pallas_call(
        functools.partial(first_kernel, per_half),
        out_shape=[
            shape((own_blocks, steps, width), bf16),
            shape((n_hi, pack_rows, width), i16),
            shape((n_hi - 1, slots, width, width), bf16),
            shape((n_hi - 1, slots, steps, width), bf16),
            shape((n_hi - 1, steps // 2, width), i32),
        ],
        in_specs=[HBM] * 6,
        out_specs=[VMEM] * 5,
        scratch_shapes=[
            pltpu.VMEM((own_blocks, steps), i32),
            pltpu.VMEM((steps, neurons), bf16),
            pltpu.SMEM((regions, slots), i32),
            pltpu.SMEM((regions, slots), i32),
            pltpu.SMEM((1, regions), i32),
            pltpu.VMEM((n_hi, slots, width, width), bf16),
            pltpu.VMEM((n_hi, slots, steps, width), bf16),
            pltpu.SemaphoreType.DMA((4 + 2 * n_hi,)),
        ],
        compiler_params=PARAMS,
        name="first_partials",
    )(
        *[
            in_hbm(x)
            for x in (block_flags.T, trace, lr_source[0, 0], lr_target[0, 0], lr_count[0], lr_weight[0, 0])
        ]
    )
    sibling = to(theirs, 1, 0)
    drive_x = to(drive, 0, 1)
    tiles, chosen, meta = rest
    mine, across = pl.pallas_call(
        second_kernel,
        out_shape=[shape((n_hi - 1, pack_rows, width), i16), shape((pack_rows, width), i16)],
        in_specs=[VMEM] * 4,
        out_specs=[VMEM] * 2,
        compiler_params=PARAMS,
        name="second_partials",
    )(chosen, meta, tiles, theirs)
    beside = to(across, 1, 1)
    merged = pl.pallas_call(
        functools.partial(merge_kernel, n_hi - 1, rows),
        out_shape=[shape((2 * rows + steps // 2, width), i16)] * (n_hi - 1),
        in_specs=[VMEM] * 2,
        out_specs=[VMEM] * (n_hi - 1),
        compiler_params=PARAMS,
        name="merge",
    )(sibling, mine)
    pair = pl.pallas_call(
        pair_kernel,
        out_shape=shape((HALVES, own_blocks, steps, width), bf16),
        in_specs=[VMEM] * 2,
        out_specs=VMEM,
        compiler_params=PARAMS,
        cost_estimate=pl.CostEstimate(flops=1 << 31, bytes_accessed=1 << 23, transcendentals=1 << 21),
        name="pair",
    )(drive, drive_x)
    arrived = []
    for k in range(1, n_hi):
        for h in range(HALVES):
            arrived.append(to(merged[k - 1], CORES * k, h))
    drive_order = [2, 3, 1] if n_far == 4 else list(range(1, n_far))
    use_order = [2, 3, 1] if n_far == 4 else list(range(1, n_far))
    sum_order = [2, 3, 1] if n_far == 4 else list(range(1, n_far))
    add_order = [1, 2, 3] if n_far == 4 else list(range(1, n_far))
    pairs = {k: to(pair, 0, k * HALVES) for k in drive_order}

    early = pl.pallas_call(
        functools.partial(early_kernel, slots),
        out_shape=shape((per_half + 1, steps, width), f32),
        in_specs=[VMEM] * 2,
        out_specs=VMEM,
        compiler_params=PARAMS,
        cost_estimate=pl.CostEstimate(flops=1 << 26, bytes_accessed=1 << 18, transcendentals=1 << 16),
        name="add_early",
    )(sibling, beside)
    far_sent = shape((own_blocks * steps + steps // 2, width), i16)
    *sums, own = pl.pallas_call(
        functools.partial(late_kernel, len(arrived), n_far, slots, own_blocks),
        out_shape=[far_sent] * (n_far - 1) + [shape((own_blocks, steps, width), f32)],
        in_specs=[VMEM] * (len(arrived) + 1),
        out_specs=[VMEM] * n_far,
        scratch_shapes=[pltpu.VMEM((per_half + 1, steps, width), f32)],
        compiler_params=PARAMS,
        cost_estimate=pl.CostEstimate(flops=1 << 37, bytes_accessed=1 << 29, transcendentals=1 << 27),
        name="add_late",
    )(early, *arrived)
    far = {k: to(sums[k - 1], 0, k * HALVES) for k in sum_order}

    inner = pl.pallas_call(
        functools.partial(inner_kernel, n_far, (0, *use_order)),
        out_shape=shape((own_blocks, steps, width), f32),
        in_specs=[VMEM] * (n_far + 1),
        out_specs=VMEM,
        compiler_params=PARAMS,
        name="inner",
    )(pair, *[pairs[k] for k in use_order], w_region[0])

    return pl.pallas_call(
        functools.partial(advance_kernel, n_far - 1),
        out_shape=[shape((steps, neurons), f32), shape((neurons,), f32)],
        in_specs=[VMEM] * (n_far + 5),
        out_specs=[VMEM] * 2,
        scratch_shapes=[pltpu.VMEM((steps, neurons), f32)],
        compiler_params=PARAMS,
        name="advance",
    )(inner, own, *[far[k] for k in add_order], g_decay, v_decay, g_start, v_start)


def solution(mesh):
    return jax.shard_map(
        functools.partial(local, mesh.shape["region"], mesh.shape["local"]),
        mesh=mesh,
        in_specs=(
            P(None, ("region", "local")),
            P(None, ("region", "local")),
            P("region", None, "local"),
            P("region", "local", None, None, None, None),
            P("region", "local", None, None),
            P("region", "local", None, None),
            P("region", "local", None),
            P(("region", "local")),
            P(("region", "local")),
            P(("region", "local")),
            P(("region", "local")),
        ),
        out_specs=(P(None, ("region", "local")), P(("region", "local"))),
        check_vma=False,
    )
```
